512 devices in a mesh: label: 64 (over y, x, core), query: 8 (over z).
Axes of the slice: x: 4, y: 8, z: 8, core: 2. Of those that a mesh axis runs over, the one named last changes fastest.
Arguments:
- queries: bfloat16 [1536, 768], P('query'), may hold values from -6 to 6
- label_ids: int32 [1536, 10], P('query'), may hold values from 0 to 4095, as said below
- label_text: bfloat16 [4096, 32, 768], P('label'), may hold values from -16 to 16
- up_weight: bfloat16 [768, 3072], P(None, 'query'), may hold values from -0.21875 to 0.21875
- down_weight: bfloat16 [768, 3072], P(None, 'query'), may hold values from -0.109375 to 0.109375
- free_vectors: float32 [4096, 768], P('label'), may hold values from -4 to 4
- moments: float32 [4096, 768], P('label'), may hold values from -0.06 to 0.06
- seconds: float32 [4096, 768], P('label'), may hold values from 1e-05 to 0.001
Outputs:
- free_new: float32 [4096, 768], P('label')
- moments_new: float32 [4096, 768], P('label')
- seconds_new: float32 [4096, 768], P('label')
- query_grad: float32 [1536, 768], P('query')
- up_grad: float32 [768, 3072], P('label', 'query')
- down_grad: float32 [768, 3072], P('label', 'query')
The draws below stay inside these ranges and needn't reach their ends.
Inputs may be any that keep to these rules, and one draw needn't show every extreme that they name: `label_ids`: the 10 ids of one query are distinct.
All inputs are finite; a program needn't handle non-finite values.
Results may differ from the reference program's by a relative error of at most 0.023.
Values sent between devices are 32-bit elements; how exact they have to be, the bound alone decides.
A program may use at most 64 MiB of HBM per device.

```python
import math
import jax
import jax.numpy as jnp
from jax import lax

D = 768
FF = 3072
K = 10
TEXT_LEN = 32
LAB_DEV = 64
LABELS = 4096
QUERIES = 1536


def draw_label_ids(key, part):
    rate_key = jax.random.fold_in(key, 11)
    pick_key = jax.random.fold_in(key, 12)
    jitter_key = jax.random.fold_in(key, 13)
    shard_count = LABELS // LAB_DEV
    column = jnp.arange(LABELS, dtype=jnp.int32)
    exponent = jax.random.randint(rate_key, (shard_count,), 0, 4)
    shard_rates = jnp.left_shift(jnp.ones((shard_count,), jnp.int32), exponent)
    label_rates = shard_rates[column // LAB_DEV]
    picked = jax.random.randint(pick_key, (LABELS,), 0, 16)
    end_labels = jnp.logical_or(column == 0, column == LABELS - 1)
    eligible = jnp.logical_or(picked < label_rates, end_labels).astype(jnp.int32)
    first_row = (jnp.arange(QUERIES, dtype=jnp.int32) == 0)[:, None]
    levels = eligible[None, :] + 2 * jnp.logical_and(first_row, end_labels[None, :]).astype(jnp.int32)
    spread = max(2, 2 ** 28 // LABELS)
    jitter = jax.random.randint(jitter_key, (QUERIES, LABELS), 0, spread)
    ranked = (levels * spread + jitter) * LABELS + column[None, :]
    chosen = lax.top_k(ranked, K)[1]
    return chosen.astype(jnp.int32)


def with_spikes(entries, rng, source, target, shards_of, factor):
    owner, partner = [(jnp.arange(entries.shape[dim]) // (entries.shape[dim] // shards_of)).reshape([-1 if axis == dim else 1 for axis in range(entries.ndim)]) for dim in (source, target)]
    chosen = jax.random.permutation(rng, shards_of)[partner]
    strong = (owner == chosen) | (owner == (partner + shards_of // 2) % shards_of)
    return jnp.where(strong, factor * entries, entries)


def level_of(rng, extent, cuts, least, largest):
    def one(position, parts):
        steps = jax.random.uniform(jax.random.fold_in(jax.random.fold_in(rng, 6), position), (parts,), jnp.float32, least / len(cuts), largest / len(cuts))
        return jnp.repeat(jnp.exp(steps), extent[position] // parts).reshape((-1,) + (1,) * (len(extent) - position - 1))

    loudness = one(*cuts[0])
    for cut in cuts[1:]:
        loudness = loudness * one(*cut)
    return loudness


def noise(stream_key, dims, deviation, bound, shards=(), kind=jnp.bfloat16):
    values = jax.random.normal(stream_key, dims, jnp.float32) * deviation
    if len(shards) > 0:
        values = level_of(stream_key, dims, shards, -0.22, 0.18) * values
    return jnp.clip(values, min=-bound, max=bound).astype(kind)


def bell_draw_with(key, shape, width, reach, cuts, heavy, kind=jnp.bfloat16):
    values = width * jax.random.normal(key, shape, jnp.float32)
    if cuts:
        values = values * level_of(key, shape, cuts, -0.22, 0.18)
    return jnp.clip(with_spikes(values, jax.random.fold_in(key, 3), *heavy), -reach, reach).astype(kind)


def setup_inputs(seed: int = 0) -> dict:
    streams_of = jax.random.split(jax.random.key(seed), 9)
    queries = noise(streams_of[0], (QUERIES, D), 1.0, 6.0, ((0, 8),))
    label_ids = draw_label_ids(jax.random.fold_in(streams_of[8], 71), 0)
    label_text = bell_draw_with(streams_of[2], (LABELS, TEXT_LEN, D), 1.0, 16.0, ((0, 64),), (0, 2, 64, 4.0))
    up_weight = noise(streams_of[3], (D, FF), D ** -0.5, 0.21875, ((1, 8),))
    down_weight = noise(streams_of[4], (D, FF), FF ** -0.5, 0.109375, ((1, 8),))
    free_vectors = noise(streams_of[5], (LABELS, D), 0.5, 4.0, ((0, 64),), jnp.float32)
    moments = noise(streams_of[6], (LABELS, D), 0.01, 0.06, ((0, 64),), jnp.float32)
    seconds = jnp.clip(jnp.exp(math.log(0.001) - 4.6051703 * jax.random.uniform(streams_of[7], (LABELS, D), jnp.float32) ** level_of(streams_of[7], (LABELS, D), ((0, 64),), -0.2, 0.2)), 9.999999747378752e-06, 0.001)
    return dict(queries=queries, label_ids=label_ids, label_text=label_text, up_weight=up_weight, down_weight=down_weight, free_vectors=free_vectors, moments=moments, seconds=seconds)


beta_one = 0.9
beta_two = 0.999
adam_eps = 1e-08
learn_rate = 0.05
first_fix = 1.0 - 0.9 ** 10
second_fix = 1.0 - 0.999 ** 10

def gelu_tanh(values):
    return jax.nn.gelu(values, approximate=True)

def reference(queries, label_ids, label_text, up_weight, down_weight, free_vectors, moments, seconds):
    temper = 1.0 / jnp.sqrt(jnp.float32(D))
    block_count = LABELS // LAB_DEV
    text_blocks = label_text.reshape(block_count, LAB_DEV, TEXT_LEN, D)

    def pool_block(text_block):
        text_rows = text_block.reshape(LAB_DEV * TEXT_LEN, D)
        preact = jnp.dot(text_rows, up_weight, preferred_element_type=jnp.float32)
        hidden = gelu_tanh(preact).astype(jnp.bfloat16)
        pooled_hidden = lax.optimization_barrier(jnp.mean(hidden.reshape(LAB_DEV, TEXT_LEN, FF), axis=1, dtype=jnp.float32))
        pooled_text = lax.optimization_barrier(jnp.mean(text_block, axis=1, dtype=jnp.float32))
        return (pooled_text, pooled_hidden)
    pooled_text, pooled_hidden = lax.map(pool_block, text_blocks)
    pooled_text = pooled_text.reshape(LABELS, D)
    pooled_hidden = pooled_hidden.reshape(LABELS, FF)
    down_float = down_weight.astype(jnp.float32)
    encoded = jnp.dot(pooled_hidden, down_float.T, precision=lax.Precision.HIGHEST)
    label_vec = pooled_text + encoded + free_vectors
    label_bf = label_vec.astype(jnp.bfloat16)
    picked = label_bf[label_ids].astype(jnp.float32)
    query_f = queries.astype(jnp.float32)
    scores = jnp.einsum('id,ikd->ik', query_f, picked) * temper
    likely = jax.nn.softmax(scores, axis=-1)
    target = jnp.where(jnp.arange(K) < 2, 0.5, 0.0).astype(jnp.float32)
    pair_coef = ((likely - target[None, :]) * temper).astype(jnp.bfloat16)
    coef_f = pair_coef.astype(jnp.float32)
    query_grad = jnp.einsum('ik,ikd->id', coef_f, picked)
    terms = (coef_f[:, :, None] * query_f[:, None, :]).reshape(-1, D)
    flat_ids = label_ids.reshape(-1).astype(jnp.int32)
    label_grad = jax.ops.segment_sum(terms, flat_ids, num_segments=LABELS)
    counts = jax.ops.segment_sum(jnp.ones(flat_ids.shape, jnp.float32), flat_ids, num_segments=LABELS)
    out_grad = label_grad.astype(jnp.bfloat16)
    down_grad = jnp.dot(out_grad.astype(jnp.float32).T, pooled_hidden, precision=lax.Precision.HIGHEST)
    hidden_grad = jnp.dot(out_grad, down_weight, preferred_element_type=jnp.float32) / TEXT_LEN
    grad_blocks = hidden_grad.reshape(block_count, LAB_DEV, FF)

    def add_block(running, pieces):
        text_block, grad_block = pieces
        text_rows = text_block.reshape(LAB_DEV * TEXT_LEN, D)
        preact = jnp.dot(text_rows, up_weight, preferred_element_type=jnp.float32)
        token_grad = jnp.broadcast_to(grad_block[:, None, :], (LAB_DEV, TEXT_LEN, FF)).reshape(LAB_DEV * TEXT_LEN, FF)
        preact_grad = jax.vjp(gelu_tanh, preact)[1](token_grad)[0].astype(jnp.bfloat16)
        return (running + jnp.dot(text_rows.T, preact_grad, preferred_element_type=jnp.float32), None)
    scanned = lax.scan(add_block, jnp.zeros((D, FF), jnp.float32), (text_blocks, grad_blocks))
    up_grad = scanned[0]
    touched = (counts > 0.5)[:, None]
    moment_step = beta_one * moments + (1.0 - beta_one) * label_grad
    second_step = beta_two * seconds + (1.0 - beta_two) * label_grad * label_grad
    update = learn_rate * (moment_step / first_fix) / (jnp.sqrt(second_step / second_fix) + adam_eps)
    free_new = jnp.where(touched, free_vectors - update, free_vectors)
    moments_new = jnp.where(touched, moment_step, moments)
    seconds_new = jnp.where(touched, second_step, seconds)
    return (free_new, moments_new, seconds_new, query_grad, up_grad, down_grad)
```

```python
import functools
import math

import jax
import jax.numpy as jnp
from jax import lax
from jax.experimental import pallas as pl
from jax.experimental.pallas import tpu as pltpu
from jax.sharding import PartitionSpec as P

MESH = pl.DeviceIdType.MESH
F32 = jnp.float32
BF16 = jnp.bfloat16

beta_one = 0.9
beta_two = 0.999
adam_eps = 1e-08
learn_rate = 0.05
first_fix = 1.0 - 0.9**10
second_fix = 1.0 - 0.999**10
ROOT = math.sqrt(2.0 / math.pi)
CUBIC = 0.044715

NT = (((1,), (1,)), ((), ()))
TN = (((0,), (0,)), ((), ()))


def far_first(count):
    return sorted(range(1, count), key=lambda o: (-min(o, count - o), o))


def kernel(
    dims,
    queries_h,
    ids_h,
    text_h,
    up_h,
    down_h,
    free_h,
    mom_h,
    sec_h,
    free_o,
    mom_o,
    sec_o,
    query_o,
    up_o,
    down_o,
    text,
    text_t,
    upw,
    dnw,
    qp,
    ids,
    fre,
    mom,
    sec,
    slope,
    pooled,
    enc,
    enc_in,
    lvec,
    lbf,
    idp,
    idt,
    idpack,
    cnt,
    cnt_in,
    sc_c,
    sc_x,
    sc_y,
    sc_c_in,
    sc_x_in,
    sc_y_in,
    lg_part,
    lg_in,
    lg,
    qt,
    q_c_in,
    q_one,
    q_x_in,
    q_two,
    q_y_in,
    q_four,
    q_five,
    q_six,
    pgrad,
    wpart,
    w_c_in,
    w_one,
    w_x_in,
    w_two,
    w_y_in,
    w_give,
    w_got,
    w_out,
    free_n,
    mom_n,
    sec_n,
    in_sem,
    text_sem,
    out_sem,
    enc_ss,
    enc_rs,
    lv_ss,
    lv_rs,
    cnt_ss,
    cnt_rs,
    sc_ss,
    sc_rs,
    lgr_ss,
    lgr_rs,
    lga_ss,
    lga_rs,
    q_ss,
    q_rs,
    w_ss,
    w_rs,
):
    ny, nx, nc, nz = dims
    lab = lax.axis_index("label")
    z = lax.axis_index("query")
    y = lab // (nx * nc)
    x = (lab // nc) % nx
    c = lab % nc
    other = 1 - c
    offs_z, offs_y, offs_x = far_first(nz), far_first(ny), far_first(nx)
    labels, width = lvec.shape
    units = upw.shape[1]
    tokens = text.shape[0] // labels
    lz = labels // nz
    rows_z = text.shape[0] // nz

    def at_z(o):
        return (lab, (z + o) % nz)

    def at_y(o):
        return (((y + o) % ny * nx + x) * nc + c, z)

    def at_x(o):
        return ((y * nx + (x + o) % nx) * nc + c, z)

    at_core = ((y * nx + x) * nc + other, z)

    barrier = pltpu.get_barrier_semaphore()
    peers = (
        [at_z(o) for o in offs_z]
        + [at_y(o) for o in offs_y]
        + [at_x(o) for o in offs_x]
        + [at_core]
    )
    for peer in peers:
        pl.semaphore_signal(barrier, inc=1, device_id=peer, device_id_type=MESH)

    def remote(src, dst, ss, rs, peer):
        return pltpu.make_async_remote_copy(
            src_ref=src,
            dst_ref=dst,
            send_sem=ss,
            recv_sem=rs,
            device_id=peer,
            device_id_type=MESH,
        )

    def offset_of(t):
        return (nz // 2 + (1 - 2 * (t % 2)) * ((t + 1) // 2)) % nz

    def text_copy(t):
        j = (z + offset_of(t)) % nz
        rows = pl.ds(pl.multiple_of(j * rows_z, rows_z), rows_z)
        return pltpu.make_async_copy(text_h.at[rows], text.at[rows], text_sem.at[t])

    in_copies = [
        pltpu.make_async_copy(src, dst, in_sem.at[i])
        for i, (src, dst) in enumerate(
            (
                (up_h, upw),
                (down_h, dnw),
                (free_h, fre),
                (ids_h, ids),
                (queries_h, qp.at[pl.ds(0, 192)]),
                (queries_h.at[pl.ds(128, 64)], qp.at[pl.ds(192, 64)]),
                (mom_h, mom),
                (sec_h, sec),
            )
        )
    ]
    in_copies[0].start()
    text_copy(0).start()
    in_copies[1].start()

    def start_text(t, carry):
        text_copy(t).start()
        return carry

    lax.fori_loop(1, nz, start_text, 0)
    for copy in in_copies[2:]:
        copy.start()
    in_copies[0].wait()

    def encode(t):
        o = offset_of(t)
        j = (z + o) % nz
        text_copy(t).wait()
        hidden = []
        for half in range(2):
            rows = pl.ds(pl.multiple_of(j * rows_z + half * (rows_z // 2), rows_z // 2), rows_z // 2)
            pre = jnp.dot(text[rows, :], upw[...], preferred_element_type=F32)
            square = pre * pre
            bent = jnp.tanh(pre * (ROOT + (ROOT * CUBIC) * square))
            gate = 0.5 + 0.5 * bent
            hidden.append(pre * gate)
            slope[rows, :] = gate + (0.5 * pre) * (1.0 - bent * bent) * (
                ROOT + (3.0 * ROOT * CUBIC) * square
            )
        hidden = jnp.concatenate(hidden, axis=0)
        mean = jnp.sum(hidden.reshape(lz, tokens, units), axis=1) * (1.0 / tokens)
        pooled[pl.ds(pl.multiple_of(j * lz, lz), lz), :] = mean
        rest = mean - mean.astype(BF16).astype(F32)
        both = jnp.concatenate([mean, rest], axis=0).astype(BF16)
        out = lax.dot_general(both, dnw[...], NT, preferred_element_type=F32)
        enc[o] = out[:lz] + out[lz:]

    def enc_copy(t):
        o = offset_of(t)
        return remote(enc.at[o], enc_in.at[o], enc_ss.at[o], enc_rs.at[o], at_z(o))

    def encode_step(t, carry):
        encode(t)
        return carry

    def send_step(t, carry):
        enc_copy(t).start()
        return carry

    def encode_send_step(t, carry):
        encode(t)
        enc_copy(t).start()
        return carry

    early = min(2, nz - 1)
    in_copies[1].wait()
    lax.fori_loop(0, early, encode_step, 0)
    pl.semaphore_wait(barrier, len(peers))
    lax.fori_loop(0, early, send_step, 0)
    lax.fori_loop(early, nz - 1, encode_send_step, 0)
    encode(nz - 1)
    own_text = pl.ds(pl.multiple_of(z * rows_z, rows_z), rows_z)
    own_rows = pl.ds(pl.multiple_of(z * lz, lz), lz)
    text_mean = jnp.sum(text[own_text, :].astype(F32).reshape(lz, tokens, width), axis=1) * (1.0 / tokens)
    in_copies[2].wait()
    total = enc[0] + text_mean + fre[own_rows, :]
    for o in offs_z:
        remote(enc.at[o], enc_in.at[o], enc_ss.at[o], enc_rs.at[o], at_z(o)).wait_recv()
        total += enc_in[o]
    lvec[own_rows, :] = total
    lv_copies = [
        remote(lvec.at[own_rows], lvec.at[own_rows], lv_ss.at[o], lv_rs.at[o], at_z(o)) for o in offs_z
    ]
    for copy in lv_copies:
        copy.start()

    in_copies[3].wait()
    idp[...] = jnp.full(idp.shape, -1.0, F32)
    local = (ids[...] - lab * labels).astype(F32)
    idp[0:192, 0:10] = local
    idp[192:256, 0:10] = local[128:192]
    idt[...] = jnp.transpose(idp[...])
    lane = lax.broadcasted_iota(jnp.int32, (1, 128), 1)
    idpack[...] = jnp.full(idpack.shape, -1.0, F32)
    idpack[0:10, :] = idt[0:10, 0:128]
    for r in range(5):
        idpack[10 + r : 11 + r, :] = jnp.where(lane < 64, idt[r : r + 1, 128:256], idt[r + 5 : r + 6, 128:256])

    def owned(p, count):
        slots = lax.broadcasted_iota(jnp.int32, (count, 128), 0).astype(F32)
        return idpack[p : p + 1, :] == slots

    def packed(rows):
        acc = jnp.zeros((128, 128), F32)
        for p in rows:
            acc += jnp.where(owned(p, 128), 1.0, 0.0)
        return acc.astype(BF16)

    ones = jnp.ones((8, 128), BF16)
    cnt[...] = lax.dot_general(ones, packed(range(10)), NT, preferred_element_type=F32) + lax.dot_general(
        ones, packed(range(10, 15)), NT, preferred_element_type=F32
    )
    cnt_copies = [remote(cnt, cnt_in.at[o], cnt_ss.at[o], cnt_rs.at[o], at_z(o)) for o in offs_z]
    for copy in cnt_copies:
        copy.start()

    def turn(t, carry):
        rows = pl.ds(pl.multiple_of(t * 256, 256), 256)
        text_t[:, rows] = jnp.transpose(text[rows, :])
        return carry

    lax.fori_loop(0, text.shape[0] // 256, turn, 0)
    in_copies[4].wait()
    in_copies[5].wait()

    for copy in lv_copies:
        copy.wait_recv()
    lbf[...] = lvec[...].astype(BF16)

    similar = lax.dot_general(lbf[...], qp[...], NT, preferred_element_type=F32)
    sc_c[...] = jnp.zeros(sc_c.shape, F32)
    for p in range(15):
        block = similar[:, 0:128] if p < 10 else similar[:, 128:256]
        sc_c[p : p + 1, :] = jnp.sum(jnp.where(owned(p, labels), block, 0.0), axis=0, keepdims=True)
    score_copies = []

    def exchange(src, dst, base, offs, at):
        copies = [
            remote(src, dst.at[o], sc_ss.at[base + o], sc_rs.at[base + o], at(o)) for o in offs
        ]
        score_copies.extend(copies)
        for copy in copies:
            copy.start()
        acc = src[...]
        for copy, o in zip(copies, offs):
            copy.wait_recv()
            acc += dst[o]
        return acc

    sc_x[...] = exchange(sc_c, sc_c_in, 0, [1], lambda o: at_core)
    sc_y[...] = exchange(sc_x, sc_x_in, 2, offs_x, at_x)
    scores = exchange(sc_y, sc_y_in, 2 + nx, offs_y, at_y)

    temper = 1.0 / math.sqrt(width)
    scores = scores * temper
    top, low = scores[0:10], scores[10:15]
    top_max = jnp.max(top, axis=0, keepdims=True)
    low_max = jnp.max(low, axis=0, keepdims=True)
    low_max = jnp.maximum(low_max, pltpu.roll(low_max, 64, 1))
    top = jnp.exp(top - top_max)
    low = jnp.exp(low - low_max)
    top_sum = jnp.sum(top, axis=0, keepdims=True)
    low_sum = jnp.sum(low, axis=0, keepdims=True)
    low_sum = low_sum + pltpu.roll(low_sum, 64, 1)
    row_t = lax.broadcasted_iota(jnp.int32, (10, 128), 0)
    row_l = lax.broadcasted_iota(jnp.int32, (5, 128), 0)
    lane_l = lax.broadcasted_iota(jnp.int32, (5, 128), 1)
    top = (top / top_sum - jnp.where(row_t < 2, 0.5, 0.0)) * temper
    low = (low / low_sum - jnp.where((row_l < 2) & (lane_l < 64), 0.5, 0.0)) * temper
    top = top.astype(BF16).astype(F32)
    low = low.astype(BF16).astype(F32)
    spread = []
    for coef, base in ((top, 0), (low, 10)):
        acc = jnp.zeros((labels, 128), F32)
        for k in range(coef.shape[0]):
            acc += jnp.where(owned(base + k, labels), coef[k : k + 1], 0.0)
        spread.append(acc)
    spread = jnp.concatenate(spread, axis=1).astype(BF16)

    lg_part[...] = jnp.dot(spread, qp[...], preferred_element_type=F32)
    lgr_copies = []
    for o in offs_z:
        rows = pl.ds(pl.multiple_of((z + o) % nz * lz, lz), lz)
        lgr_copies.append(remote(lg_part.at[rows], lg_in.at[o], lgr_ss.at[o], lgr_rs.at[o], at_z(o)))
        lgr_copies[-1].start()

    terms = lax.dot_general(spread, lbf[...], TN, preferred_element_type=F32)
    for half in range(2):
        cols = slice(half * (width // 2), (half + 1) * (width // 2))
        qt[half, 0:128, :] = terms[0:128, cols]
        qt[half, 128:192, :] = terms[128:192, cols] + terms[192:256, cols]
    q_core = remote(qt.at[other], q_c_in, q_ss.at[0], q_rs.at[0], at_core)
    q_core.start()
    qx = 192 // nx
    owners = 6 if ny == 8 else ny
    qy = qx // owners
    q_core.wait_recv()
    q_one[...] = qt[c] + q_c_in[...]
    q_x_copies = []
    for o in offs_x:
        rows = pl.ds(pl.multiple_of((x + o) % nx * qx, qx), qx)
        q_x_copies.append(remote(q_one.at[rows], q_x_in.at[o], q_ss.at[1 + o], q_rs.at[1 + o], at_x(o)))
        q_x_copies[-1].start()

    total = lg_part[own_rows, :]
    for copy, o in zip(lgr_copies, offs_z):
        copy.wait_recv()
        total += lg_in[o]
    lg[own_rows, :] = total
    lga_copies = [remote(lg.at[own_rows], lg.at[own_rows], lga_ss.at[o], lga_rs.at[o], at_z(o)) for o in offs_z]
    for copy in lga_copies:
        copy.start()

    acc = q_one[pl.ds(pl.multiple_of(x * qx, qx), qx), :]
    for copy, o in zip(q_x_copies, offs_x):
        copy.wait_recv()
        acc += q_x_in[o]
    q_two[...] = acc
    base_y = 1 + nx
    base_g = base_y + ny

    def q_y_copy(b):
        o = (b - y + ny) % ny
        return o, remote(
            q_two.at[pl.ds(b * qy, qy)],
            q_y_in.at[o],
            q_ss.at[base_y + b],
            q_rs.at[base_y + o],
            ((b * nx + x) * nc + c, z),
        )

    for b in range(owners):
        o, copy = q_y_copy(b)

        @pl.when(o != 0)
        def _():
            copy.start()

    seen = cnt[...]
    for copy, o in zip(cnt_copies, offs_z):
        copy.wait_recv()
        seen += cnt_in[o]
    diag = lax.broadcasted_iota(jnp.int32, (labels, 128), 0) == lax.broadcasted_iota(
        jnp.int32, (labels, 128), 1
    )
    touched = jnp.sum(jnp.where(diag, seen[0:1], 0.0), axis=1, keepdims=True) > 0.5

    for copy in lga_copies:
        copy.wait_recv()
    grad = lg[...]
    out_grad = grad.astype(BF16)
    hidden_grad = jnp.dot(out_grad, dnw[...], preferred_element_type=F32) * (1.0 / tokens)

    mean = pooled[...]
    rest = mean - mean.astype(BF16).astype(F32)
    both = jnp.concatenate([mean, rest], axis=0).astype(BF16)
    twice = jnp.concatenate([out_grad, out_grad], axis=0)
    down_part = lax.dot_general(twice, both, TN, preferred_element_type=F32)
    wpart[0] = down_part.reshape(wpart.shape[1:])
    w_core = [remote(wpart.at[k, other], w_c_in.at[k], w_ss.at[k, 0], w_rs.at[k, 0], at_core) for k in range(2)]
    w_core[0].start()

    for j in range(nz):
        rows = slice(j * rows_z, (j + 1) * rows_z)
        spreaded = jnp.broadcast_to(
            hidden_grad[j * lz : (j + 1) * lz, None, :], (lz, tokens, units)
        ).reshape(rows_z, units)
        pgrad[rows, :] = (slope[rows, :] * spreaded).astype(BF16)

    half_rows = width // nc

    def up_half(h):
        rows = pl.ds(pl.multiple_of(h * half_rows, half_rows), half_rows)
        part = jnp.dot(text_t[rows, :], pgrad[...], preferred_element_type=F32)
        wpart[1, h] = part.reshape(wpart.shape[2:])

    up_half(other)
    w_core[1].start()

    w_x_copies = [[], []]

    def across_x(k):
        w_core[k].wait_recv()
        w_one[k] = wpart[k, c] + w_c_in[k]
        for o in offs_x:
            copy = remote(
                w_one.at[k, :, (x + o) % nx],
                w_x_in.at[k, o],
                w_ss.at[k, 1 + o],
                w_rs.at[k, 1 + o],
                at_x(o),
            )
            copy.start()
            w_x_copies[k].append(copy)

    across_x(0)
    up_half(c)
    across_x(1)

    @pl.when(y < owners)
    def _():
        acc = q_two[pl.ds(pl.multiple_of(y % owners * qy, qy), qy), :]
        for o in offs_y:
            remote(
                q_two.at[pl.ds(0, qy)], q_y_in.at[o], q_ss.at[base_y], q_rs.at[base_y + o], at_y(o)
            ).wait_recv()
            acc += q_y_in[o]
        mine = pl.ds(pl.multiple_of(y % owners * qy, qy), qy)
        q_four[mine, :] = acc
        for o in offs_y:
            remote(
                q_four.at[mine], q_four.at[mine], q_ss.at[base_g + o], q_rs.at[base_g + y], at_y(o)
            ).start()

    in_copies[6].wait()
    in_copies[7].wait()
    moment = beta_one * mom[...] + (1.0 - beta_one) * grad
    second = beta_two * sec[...] + (1.0 - beta_two) * grad * grad
    update = learn_rate * (moment / first_fix) / (jnp.sqrt(second / second_fix) + adam_eps)
    free_n[...] = jnp.where(touched, fre[...] - update, fre[...])
    mom_n[...] = jnp.where(touched, moment, mom[...])
    sec_n[...] = jnp.where(touched, second, sec[...])
    out_copies = [
        pltpu.make_async_copy(src, dst, out_sem.at[i])
        for i, (src, dst) in enumerate(((free_n, free_o), (mom_n, mom_o), (sec_n, sec_o)))
    ]
    for copy in out_copies:
        copy.start()

    for b in range(owners):

        @pl.when(y != b)
        def _():
            rows = pl.ds(b * qy, qy)
            remote(
                q_four.at[rows], q_four.at[rows], q_ss.at[base_g], q_rs.at[base_g + b], at_core
            ).wait_recv()

    own_x = pl.ds(pl.multiple_of(x * qx, qx), qx)
    q_five[own_x, :] = q_four[...]
    base_h = base_g + ny
    q_xg_copies = [
        remote(q_four, q_five.at[own_x], q_ss.at[base_h + o], q_rs.at[base_h + o], at_x(o)) for o in offs_x
    ]
    for copy in q_xg_copies:
        copy.start()

    per_core = ny // nc

    def w_y_copy(k, b):
        goal = c * per_core + b
        o = (goal - y + ny) % ny
        return o, remote(
            w_two.at[k, b],
            w_y_in.at[k, o],
            w_ss.at[k, 1 + nx + b],
            w_rs.at[k, 1 + nx + o],
            ((goal * nx + x) * nc + c, z),
        )

    def across_y(k):
        acc = w_one[k, :, x]
        for copy, o in zip(w_x_copies[k], offs_x):
            copy.wait_recv()
            acc += w_x_in[k, o]
        w_two[k] = acc
        for b in range(per_core):
            o, copy = w_y_copy(k, b)

            @pl.when(o != 0)
            def _():
                copy.start()

    across_y(0)
    across_y(1)

    for copy in q_xg_copies:
        copy.wait_recv()
    q_back = remote(q_five, q_six, q_ss.at[base_h + nx], q_rs.at[base_h + nx], at_core)
    q_back.start()

    holder = y // per_core == c
    rows_out = w_out.shape[1]

    def w_last(k):
        return remote(
            w_give.at[k], w_got.at[k], w_ss.at[k, 1 + nx + ny], w_rs.at[k, 1 + nx + ny], at_core
        )

    for k in range(2):

        @pl.when(holder)
        def _():
            acc = w_two[k, y % per_core]
            for o in offs_y:
                remote(
                    w_two.at[k, 0], w_y_in.at[k, o], w_ss.at[k, 0], w_rs.at[k, 1 + nx + o], at_y(o)
                ).wait_recv()
                acc += w_y_in[k, o]
            first, last = acc[:rows_out], acc[rows_out:]
            w_give[k, 0:rows_out, :] = jnp.where(c == 0, last, first)
            w_last(k).start()
            w_out[k] = jnp.where(c == 0, first, last)

    for half in range(2):
        cols = slice(half * (width // 2), (half + 1) * (width // 2))

        @pl.when(c == half)
        def _():
            pltpu.make_async_copy(q_five, query_o.at[:, cols], out_sem.at[3]).start()

    q_back.wait_recv()
    for half in range(2):
        cols = slice(half * (width // 2), (half + 1) * (width // 2))

        @pl.when(other == half)
        def _():
            pltpu.make_async_copy(q_six, query_o.at[:, cols], out_sem.at[4]).start()

    for k in range(2):

        @pl.when(jnp.logical_not(holder))
        def _():
            w_last(k).wait_recv()
            w_out[k] = w_got[k, 0:rows_out, :]

    w_writes = [
        pltpu.make_async_copy(w_out.at[0], down_o, out_sem.at[5]),
        pltpu.make_async_copy(w_out.at[1], up_o, out_sem.at[6]),
    ]
    for copy in w_writes:
        copy.start()

    for o in offs_z:
        remote(enc.at[o], enc_in.at[o], enc_ss.at[o], enc_rs.at[o], at_z(o)).wait_send()
    for copy in (
        lv_copies + cnt_copies + score_copies + lgr_copies + lga_copies + q_x_copies + q_xg_copies
        + w_core + w_x_copies[0] + w_x_copies[1] + [q_core, q_back]
    ):
        copy.wait_send()
    for b in range(owners):
        o, copy = q_y_copy(b)

        @pl.when(o != 0)
        def _():
            copy.wait_send()

    @pl.when(y < owners)
    def _():
        mine = pl.ds(pl.multiple_of(y % owners * qy, qy), qy)
        for o in offs_y:
            remote(
                q_four.at[mine], q_four.at[mine], q_ss.at[base_g + o], q_rs.at[base_g + y], at_y(o)
            ).wait_send()

    for k in range(2):
        for b in range(per_core):
            o, copy = w_y_copy(k, b)

            @pl.when(o != 0)
            def _():
                copy.wait_send()

        @pl.when(holder)
        def _():
            w_last(k).wait_send()

    for copy in out_copies + w_writes:
        copy.wait()
    pltpu.make_async_copy(q_five, query_o.at[:, 0 : width // 2], out_sem.at[3]).wait()
    pltpu.make_async_copy(q_six, query_o.at[:, 0 : width // 2], out_sem.at[4]).wait()


def body(dims, queries, label_ids, label_text, up_weight, down_weight, free_vectors, moments, seconds):
    ny, nx, nc, nz = dims
    labels, tokens, width = label_text.shape
    units = up_weight.shape[1]
    rows = labels * tokens
    text_rows = label_text.reshape(rows, width)
    lz = labels // nz
    rows_out = width // (ny * nx * nc)
    chip_rows = rows_out * nc
    per_core = ny // nc
    half = width // 2
    qx = 192 // nx
    qy = qx // (6 if ny == 8 else ny)
    staged = -(-rows_out // 8) * 8
    vmem = pltpu.VMEM
    dma = pltpu.SemaphoreType.DMA
    scratch = [
        vmem((rows, width), BF16),
        vmem((width, rows), BF16),
        vmem((width, units), BF16),
        vmem((width, units), BF16),
        vmem((256, width), BF16),
        vmem((192, 10), jnp.int32),
        vmem((labels, width), F32),
        vmem((labels, width), F32),
        vmem((labels, width), F32),
        vmem((rows, units), F32),
        vmem((labels, units), F32),
        vmem((nz, lz, width), F32),
        vmem((nz, lz, width), F32),
        vmem((labels, width), F32),
        vmem((labels, width), BF16),
        vmem((256, 128), F32),
        vmem((128, 256), F32),
        vmem((16, 128), F32),
        vmem((8, 128), F32),
        vmem((nz, 8, 128), F32),
        vmem((16, 128), F32),
        vmem((16, 128), F32),
        vmem((16, 128), F32),
        vmem((2, 16, 128), F32),
        vmem((nx, 16, 128), F32),
        vmem((ny, 16, 128), F32),
        vmem((labels, width), F32),
        vmem((nz, lz, width), F32),
        vmem((labels, width), F32),
        vmem((2, 192, half), F32),
        vmem((192, half), F32),
        vmem((192, half), F32),
        vmem((nx, qx, half), F32),
        vmem((qx, half), F32),
        vmem((ny, qy, half), F32),
        vmem((qx, half), F32),
        vmem((192, half), F32),
        vmem((192, half), F32),
        vmem((rows, units), BF16),
        vmem((2, nc, per_core, nx, chip_rows, units), F32),
        vmem((2, per_core, nx, chip_rows, units), F32),
        vmem((2, per_core, nx, chip_rows, units), F32),
        vmem((2, nx, per_core, chip_rows, units), F32),
        vmem((2, per_core, chip_rows, units), F32),
        vmem((2, ny, chip_rows, units), F32),
        vmem((2, staged, units), F32),
        vmem((2, staged, units), F32),
        vmem((2, rows_out, units), F32),
        vmem((labels, width), F32),
        vmem((labels, width), F32),
        vmem((labels, width), F32),
        dma((8,)),
        dma((nz,)),
        dma((7,)),
        dma((nz,)),
        dma((nz,)),
        dma((nz,)),
        dma((nz,)),
        dma((nz,)),
        dma((nz,)),
        dma((2 + nx + ny,)),
        dma((2 + nx + ny,)),
        dma((nz,)),
        dma((nz,)),
        dma((nz,)),
        dma((nz,)),
        dma((2 + 2 * nx + 2 * ny,)),
        dma((2 + 2 * nx + 2 * ny,)),
        dma((2, 2 + nx + ny)),
        dma((2, 2 + nx + ny)),
    ]
    hbm = pl.BlockSpec(memory_space=pl.ANY)
    flops = 2 * rows * width * units * 2
    return pl.pallas_call(
        functools.partial(kernel, dims),
        out_shape=[
            jax.ShapeDtypeStruct((labels, width), F32),
            jax.ShapeDtypeStruct((labels, width), F32),
            jax.ShapeDtypeStruct((labels, width), F32),
            jax.ShapeDtypeStruct((192, width), F32),
            jax.ShapeDtypeStruct((rows_out, units), F32),
            jax.ShapeDtypeStruct((rows_out, units), F32),
        ],
        in_specs=[hbm] * 8,
        out_specs=[hbm] * 6,
        scratch_shapes=scratch,
        name="step",
        cost_estimate=pl.CostEstimate(flops=flops, bytes_accessed=8 * 2**20, transcendentals=rows * units),
        compiler_params=pltpu.CompilerParams(
            collective_id=0, has_side_effects=True, vmem_limit_bytes=56 * 2**20
        ),
    )(queries, label_ids, text_rows, up_weight, down_weight, free_vectors, moments, seconds)


def build(mesh, dims):
    placed = (
        P("query", None),
        P("query", None),
        P("label", None, None),
        P(None, "query"),
        P(None, "query"),
        P("label", None),
        P("label", None),
        P("label", None),
    )
    return jax.shard_map(
        functools.partial(body, dims),
        mesh=mesh,
        in_specs=placed,
        out_specs=(
            P("label", None),
            P("label", None),
            P("label", None),
            P("query", None),
            P("label", "query"),
            P("label", "query"),
        ),
        check_vma=False,
    )


def solution(mesh):
    return build(mesh, (8, 4, 2, mesh.shape["query"]))
```

```python
import functools
import math

import jax
import jax.numpy as jnp
from jax import lax
from jax.experimental import pallas as pl
from jax.experimental.pallas import tpu as pltpu
from jax.sharding import PartitionSpec as P

MESH = pl.DeviceIdType.MESH
F32 = jnp.float32
BF16 = jnp.bfloat16

beta_one = 0.9
beta_two = 0.999
adam_eps = 1e-08
learn_rate = 0.05
first_fix = 1.0 - 0.9**10
second_fix = 1.0 - 0.999**10
ROOT = math.sqrt(2.0 / math.pi)
CUBIC = 0.044715

NT = (((1,), (1,)), ((), ()))
TN = (((0,), (0,)), ((), ()))


def far_first(count):
    return sorted(range(1, count), key=lambda o: (-min(o, count - o), o))


def kernel(
    dims,
    queries_h,
    ids_h,
    text_h,
    up_h,
    down_h,
    free_h,
    mom_h,
    sec_h,
    free_o,
    mom_o,
    sec_o,
    query_o,
    up_o,
    down_o,
    text,
    text_t,
    upw,
    dnw,
    qp,
    ids,
    fre,
    mom,
    sec,
    slope,
    pool_in,
    pool_bf,
    enc,
    enc_in,
    lvec,
    lbf,
    idp,
    idt,
    idpack,
    cnt,
    cnt_in,
    sc_c,
    sc_x,
    sc_y,
    sc_c_in,
    sc_x_in,
    sc_y_in,
    lg_part,
    lg_in,
    lg,
    qt,
    q_c_in,
    q_one,
    q_y_in,
    q_x_in,
    q_five,
    q_six,
    lg_pair,
    og_t,
    og_in,
    pgrad,
    upart,
    u_c_in,
    u_one,
    u_x_in,
    w_two,
    w_y_in,
    w_out,
    free_n,
    mom_n,
    sec_n,
    in_sem,
    text_sem,
    out_sem,
    enc_ss,
    enc_rs,
    lv_ss,
    lv_rs,
    cnt_ss,
    cnt_rs,
    sc_ss,
    sc_rs,
    lgr_ss,
    lgr_rs,
    lga_ss,
    lga_rs,
    q_ss,
    q_rs,
    pool_ss,
    pool_rs,
    og_ss,
    og_rs,
    u_ss,
    u_rs,
    w_ss,
    w_rs,
):
    ny, nx, nc, nz = dims
    lab = lax.axis_index("label")
    z = lax.axis_index("query")
    y = lab // (nx * nc)
    x = (lab // nc) % nx
    c = lab % nc
    other = 1 - c
    offs_z, offs_y, offs_x = far_first(nz), far_first(ny), far_first(nx)
    labels, width = lvec.shape
    units = upw.shape[1]
    tokens = text.shape[0] // labels
    lz = labels // nz
    rows_z = text.shape[0] // nz

    def at_z(o):
        return (lab, (z + o) % nz)

    def at_y(o):
        return (((y + o) % ny * nx + x) * nc + c, z)

    def at_x(o):
        return ((y * nx + (x + o) % nx) * nc + c, z)

    def at_y_other(o):
        return (((y + o) % ny * nx + x) * nc + other, z)

    at_core = ((y * nx + x) * nc + other, z)

    barrier = pltpu.get_barrier_semaphore()
    peers = (
        [at_z(o) for o in offs_z]
        + [at_y(o) for o in offs_y]
        + [at_y_other(o) for o in offs_y]
        + [at_x(o) for o in offs_x]
        + [at_core]
    )
    for peer in peers:
        pl.semaphore_signal(barrier, inc=1, device_id=peer, device_id_type=MESH)

    def remote(src, dst, ss, rs, peer):
        return pltpu.make_async_remote_copy(
            src_ref=src,
            dst_ref=dst,
            send_sem=ss,
            recv_sem=rs,
            device_id=peer,
            device_id_type=MESH,
        )

    def offset_of(t):
        return (nz // 2 + (1 - 2 * (t % 2)) * ((t + 1) // 2)) % nz

    def text_copy(t):
        j = (z + offset_of(t)) % nz
        rows = pl.ds(pl.multiple_of(j * rows_z, rows_z), rows_z)
        return pltpu.make_async_copy(text_h.at[rows], text.at[rows], text_sem.at[t])

    in_copies = [
        pltpu.make_async_copy(src, dst, in_sem.at[i])
        for i, (src, dst) in enumerate(
            (
                (up_h, upw),
                (down_h, dnw),
                (free_h, fre),
                (ids_h, ids),
                (queries_h, qp.at[pl.ds(0, 192)]),
                (queries_h.at[pl.ds(128, 64)], qp.at[pl.ds(192, 64)]),
                (mom_h, mom),
                (sec_h, sec),
            )
        )
    ]
    in_copies[0].start()
    text_copy(0).start()
    in_copies[1].start()

    def start_text(t, carry):
        text_copy(t).start()
        return carry

    lax.fori_loop(1, nz, start_text, 0)
    for copy in in_copies[2:]:
        copy.start()
    in_copies[0].wait()

    def encode(t):
        o = offset_of(t)
        j = (z + o) % nz
        text_copy(t).wait()
        hidden = []
        for half in range(2):
            rows = pl.ds(pl.multiple_of(j * rows_z + half * (rows_z // 2), rows_z // 2), rows_z // 2)
            pre = jnp.dot(text[rows, :], upw[...], preferred_element_type=F32)
            square = pre * pre
            bent = jnp.tanh(pre * (ROOT + (ROOT * CUBIC) * square))
            gate = 0.5 + 0.5 * bent
            hidden.append(pre * gate)
            slope[rows, :] = gate + (0.5 * pre) * (1.0 - bent * bent) * (
                ROOT + (3.0 * ROOT * CUBIC) * square
            )
        hidden = jnp.concatenate(hidden, axis=0)
        mean = jnp.sum(hidden.reshape(lz, tokens, units), axis=1) * (1.0 / tokens)
        pool_in[0, c, pl.ds(pl.multiple_of(j * lz, lz), lz), :] = mean
        rest = mean - mean.astype(BF16).astype(F32)
        both = jnp.concatenate([mean, rest], axis=0).astype(BF16)
        out = lax.dot_general(both, dnw[...], NT, preferred_element_type=F32)
        enc[o] = out[:lz] + out[lz:]

    def enc_copy(t):
        o = offset_of(t)
        return remote(enc.at[o], enc_in.at[o], enc_ss.at[o], enc_rs.at[o], at_z(o))

    def encode_step(t, carry):
        encode(t)
        return carry

    def send_step(t, carry):
        enc_copy(t).start()
        return carry

    def encode_send_step(t, carry):
        encode(t)
        enc_copy(t).start()
        return carry

    early = min(5, nz - 1)
    in_copies[1].wait()
    lax.fori_loop(0, early, encode_step, 0)
    pl.semaphore_wait(barrier, len(peers))
    lax.fori_loop(0, early, send_step, 0)
    lax.fori_loop(early, nz - 1, encode_send_step, 0)
    encode(nz - 1)
    own_text = pl.ds(pl.multiple_of(z * rows_z, rows_z), rows_z)
    own_rows = pl.ds(pl.multiple_of(z * lz, lz), lz)
    text_mean = jnp.sum(text[own_text, :].astype(F32).reshape(lz, tokens, width), axis=1) * (1.0 / tokens)
    in_copies[2].wait()
    total = enc[0] + text_mean + fre[own_rows, :]
    for o in offs_z:
        remote(enc.at[o], enc_in.at[o], enc_ss.at[o], enc_rs.at[o], at_z(o)).wait_recv()
        total += enc_in[o]
    lvec[own_rows, :] = total
    lv_copies = [
        remote(lvec.at[own_rows], lvec.at[own_rows], lv_ss.at[o], lv_rs.at[o], at_z(o)) for o in offs_z
    ]
    for copy in lv_copies:
        copy.start()
    pool_copies = [remote(pool_in.at[0, c], pool_in.at[0, c], pool_ss.at[0], pool_rs.at[0], at_core)]
    pool_copies += [
        remote(pool_in.at[0, c], pool_in.at[o, c], pool_ss.at[o], pool_rs.at[o], at_x(o)) for o in offs_x
    ]
    for copy in pool_copies:
        copy.start()

    in_copies[3].wait()
    local = (ids[...] - lab * labels).astype(F32)
    idp[...] = jnp.full(idp.shape, -1.0, F32)
    idp[0:10, 0:64] = local[:, 128:192]
    idt[...] = pltpu.roll(idp[...], 64, 1)
    lane = lax.broadcasted_iota(jnp.int32, (1, 128), 1)
    idpack[...] = jnp.full(idpack.shape, -1.0, F32)
    idpack[0:10, :] = local[:, 0:128]
    for r in range(5):
        idpack[10 + r : 11 + r, :] = jnp.where(lane < 64, idp[r : r + 1, :], idt[r + 5 : r + 6, :])

    def owned(p, count):
        slots = lax.broadcasted_iota(jnp.int32, (count, 128), 0).astype(F32)
        return idpack[p : p + 1, :] == slots

    def packed(rows):
        acc = jnp.zeros((128, 128), F32)
        for p in rows:
            acc += jnp.where(owned(p, 128), 1.0, 0.0)
        return acc.astype(BF16)

    ones = jnp.ones((8, 128), BF16)
    cnt[...] = lax.dot_general(ones, packed(range(10)), NT, preferred_element_type=F32) + lax.dot_general(
        ones, packed(range(10, 15)), NT, preferred_element_type=F32
    )
    cnt_copies = [remote(cnt, cnt_in.at[o], cnt_ss.at[o], cnt_rs.at[o], at_z(o)) for o in offs_z]
    for copy in cnt_copies:
        copy.start()

    def turn(t, carry):
        rows = pl.ds(pl.multiple_of(t * 256, 256), 256)
        text_t[:, rows] = jnp.transpose(text[rows, :])
        return carry

    turns = text.shape[0] // 256
    in_copies[4].wait()
    in_copies[5].wait()

    for copy in lv_copies:
        copy.wait_recv()
    lbf[...] = lvec[...].astype(BF16)

    similar = lax.dot_general(lbf[...], qp[...], NT, preferred_element_type=F32)
    sc_c[...] = jnp.zeros(sc_c.shape, F32)
    for p in range(15):
        block = similar[:, 0:128] if p < 10 else similar[:, 128:256]
        sc_c[p : p + 1, :] = jnp.sum(jnp.where(owned(p, labels), block, 0.0), axis=0, keepdims=True)
    score_copies = []

    def exchange(src, dst, base, offs, at, first, last):
        copies = [
            remote(src, dst.at[o], sc_ss.at[base + o], sc_rs.at[base + o], at(o)) for o in offs
        ]
        score_copies.extend(copies)
        for copy in copies:
            copy.start()
        lax.fori_loop(first, last, turn, 0)
        acc = src[...]
        for copy, o in zip(copies, offs):
            copy.wait_recv()
            acc += dst[o]
        return acc

    sc_x[...] = exchange(sc_c, sc_c_in, 0, [1], lambda o: at_core, 0, 0)
    sc_y[...] = exchange(sc_x, sc_x_in, 2, offs_x, at_x, 0, turns // 4)
    scores = exchange(sc_y, sc_y_in, 2 + nx, offs_y, at_y, turns // 4, turns)

    temper = 1.0 / math.sqrt(width)
    scores = scores * temper
    top, low = scores[0:10], scores[10:15]
    top_max = jnp.max(top, axis=0, keepdims=True)
    low_max = jnp.max(low, axis=0, keepdims=True)
    low_max = jnp.maximum(low_max, pltpu.roll(low_max, 64, 1))
    top = jnp.exp(top - top_max)
    low = jnp.exp(low - low_max)
    top_sum = jnp.sum(top, axis=0, keepdims=True)
    low_sum = jnp.sum(low, axis=0, keepdims=True)
    low_sum = low_sum + pltpu.roll(low_sum, 64, 1)
    row_t = lax.broadcasted_iota(jnp.int32, (10, 128), 0)
    row_l = lax.broadcasted_iota(jnp.int32, (5, 128), 0)
    lane_l = lax.broadcasted_iota(jnp.int32, (5, 128), 1)
    top = (top / top_sum - jnp.where(row_t < 2, 0.5, 0.0)) * temper
    low = (low / low_sum - jnp.where((row_l < 2) & (lane_l < 64), 0.5, 0.0)) * temper
    top = top.astype(BF16).astype(F32)
    low = low.astype(BF16).astype(F32)
    spread = []
    for coef, base in ((top, 0), (low, 10)):
        acc = jnp.zeros((labels, 128), F32)
        for k in range(coef.shape[0]):
            acc += jnp.where(owned(base + k, labels), coef[k : k + 1], 0.0)
        spread.append(acc)
    spread = jnp.concatenate(spread, axis=1).astype(BF16)

    lg_part[...] = jnp.dot(spread, qp[...], preferred_element_type=F32)
    lgr_copies = []
    for o in offs_z:
        rows = pl.ds(pl.multiple_of((z + o) % nz * lz, lz), lz)
        lgr_copies.append(remote(lg_part.at[rows], lg_in.at[o], lgr_ss.at[o], lgr_rs.at[o], at_z(o)))
        lgr_copies[-1].start()

    terms = lax.dot_general(spread, lbf[...], TN, preferred_element_type=F32)
    for half in range(2):
        cols = slice(half * (width // 2), (half + 1) * (width // 2))
        qt[half, 0:128, :] = terms[0:128, cols]
        qt[half, 128:192, :] = terms[128:192, cols] + terms[192:256, cols]
    q_core = remote(qt.at[other], q_c_in, q_ss.at[0], q_rs.at[0], at_core)
    q_core.start()
    pool_back = []
    for copy, o in zip(pool_copies[1:], offs_x):
        copy.wait_recv()
        pool_back.append(
            remote(pool_in.at[o, c], pool_in.at[o, c], pool_ss.at[nx + o], pool_rs.at[nx + o], at_core)
        )
        pool_back[-1].start()
    qy = 192 // ny
    base_x, base_g = 1 + ny, 1 + ny + nx
    q_core.wait_recv()
    q_one[...] = qt[c] + q_c_in[...]
    q_y_copies = []
    for o in offs_y:
        rows = pl.ds(pl.multiple_of((y + o) % ny * qy, qy), qy)
        q_y_copies.append(remote(q_one.at[rows], q_y_in.at[o], q_ss.at[1 + o], q_rs.at[1 + o], at_y(o)))
        q_y_copies[-1].start()

    total = lg_part[own_rows, :]
    for copy, o in zip(lgr_copies, offs_z):
        copy.wait_recv()
        total += lg_in[o]
    lg[own_rows, :] = total
    lga_copies = [remote(lg.at[own_rows], lg.at[own_rows], lga_ss.at[o], lga_rs.at[o], at_z(o)) for o in offs_z]
    for copy in lga_copies:
        copy.start()

    seen = cnt[...]
    for copy, o in zip(cnt_copies, offs_z):
        copy.wait_recv()
        seen += cnt_in[o]
    diag = lax.broadcasted_iota(jnp.int32, (labels, 128), 0) == lax.broadcasted_iota(
        jnp.int32, (labels, 128), 1
    )
    touched = jnp.sum(jnp.where(diag, seen[0:1], 0.0), axis=1, keepdims=True) > 0.5

    pool_copies[0].wait_recv()
    for copy in pool_back:
        copy.wait_recv()
    for o in range(nx):
        for k in range(nc):
            mean = pool_in[o, k]
            whole = mean.astype(BF16)
            pool_bf[o, k * labels : (k + 1) * labels, :] = whole
            pool_bf[o, (nc + k) * labels : (nc + k + 1) * labels, :] = (mean - whole.astype(F32)).astype(BF16)

    for copy in lga_copies:
        copy.wait_recv()
    grad = lg[...]
    out_grad = grad.astype(BF16)
    hidden_grad = jnp.dot(out_grad, dnw[...], preferred_element_type=F32) * (1.0 / tokens)

    half_rows = width // nc
    cols_other = pl.ds(pl.multiple_of(other * half_rows, half_rows), half_rows)
    og_core = remote(lg.at[:, cols_other], lg_pair.at[c], og_ss.at[0], og_rs.at[0], at_core)
    og_core.start()

    own_y = pl.ds(pl.multiple_of(y * qy, qy), qy)
    acc = q_one[own_y, :]
    for copy, o in zip(q_y_copies, offs_y):
        copy.wait_recv()
        acc += q_y_in[o]
    q_x_in[x] = acc
    q_x_copies = [
        remote(q_x_in.at[x], q_x_in.at[x], q_ss.at[base_x + o], q_rs.at[base_x + o], at_x(o)) for o in offs_x
    ]
    for copy in q_x_copies:
        copy.start()

    lg_pair[c] = jnp.where(c == 0, grad[:, :half_rows], grad[:, half_rows:])
    for j in range(nz):
        rows = slice(j * rows_z, (j + 1) * rows_z)
        spreaded = jnp.broadcast_to(
            hidden_grad[j * lz : (j + 1) * lz, None, :], (lz, tokens, units)
        ).reshape(rows_z, units)
        pgrad[rows, :] = (slope[rows, :] * spreaded).astype(BF16)

    og_core.wait_recv()
    pair = lg_pair[...].reshape(nc * labels, half_rows).astype(BF16).astype(F32)
    og_t[...] = jnp.transpose(pair).reshape(og_t.shape)
    og_copies = []
    for o in offs_x:
        og_copies.append(
            remote(og_t.at[:, (x + o) % nx], og_in.at[o], og_ss.at[1 + o], og_rs.at[1 + o], at_x(o))
        )
        og_copies[-1].start()

    per_core = ny // nc
    pieces = 2 if per_core % 2 == 0 else 1
    per_piece = per_core // pieces
    piece_rows = half_rows // pieces

    def up_piece(h, p):
        rows = pl.ds(pl.multiple_of(h * half_rows + p * piece_rows, piece_rows), piece_rows)
        part = jnp.dot(text_t[rows, :], pgrad[...], preferred_element_type=F32)
        upart[h, p] = part.reshape(upart.shape[2:])

    u_core = []
    for p in range(pieces):
        up_piece(other, p)
        u_core.append(remote(upart.at[other, p], u_c_in.at[p], u_ss.at[p, 0], u_rs.at[p, 0], at_core))
        u_core[p].start()

    u_x_copies = [[], []]

    def across_x(p):
        u_core[p].wait_recv()
        u_one[p] = upart[c, p] + u_c_in[p]
        for o in offs_x:
            copy = remote(
                u_one.at[p, :, (x + o) % nx],
                u_x_in.at[p, o],
                u_ss.at[p, 1 + o],
                u_rs.at[p, 1 + o],
                at_x(o),
            )
            copy.start()
            u_x_copies[p].append(copy)

    for p in range(pieces):
        up_piece(c, p)
        across_x(p)

    rows_out = w_out.shape[1]
    step_rows, slice_rows = rows_out // 8 * 8, -(-rows_out // 8) * 8

    def w_y_copies(k, b):
        goal = c * per_core + b
        o = (goal - y + ny) % ny
        copies = []
        for side, core in enumerate((c, other)):
            rows = pl.ds(pl.multiple_of(core * step_rows, 8), slice_rows)
            copies.append(
                remote(
                    w_two.at[k, b, rows],
                    w_y_in.at[k, o],
                    w_ss.at[k, side, b],
                    w_rs.at[k, o],
                    ((goal * nx + x) * nc + core, z),
                )
            )
        return o, copies

    def across_y(k, b):
        o, copies = w_y_copies(k, b)
        copies[1].start()

        @pl.when(o != 0)
        def _():
            copies[0].start()

        @pl.when(o == 0)
        def _():
            w_y_in[k, 0] = w_two[k, b, pl.ds(pl.multiple_of(c * step_rows, 8), slice_rows), :]

    def down_term(values, o):
        values = values.reshape(half_rows // nx, nc * labels).astype(BF16)
        return jnp.dot(
            jnp.concatenate([values, values], axis=1), pool_bf[o], preferred_element_type=F32
        )

    acc = down_term(og_t[:, x], 0)
    for copy, o in zip(og_copies, offs_x):
        copy.wait_recv()
        acc += down_term(og_in[o], o)
    w_two[0] = acc.reshape(w_two.shape[1:])
    for b in range(per_core):
        across_y(0, b)

    for copy in q_x_copies:
        copy.wait_recv()
    acc = q_x_in[0]
    for i in range(1, nx):
        acc += q_x_in[i]
    q_five[own_y, :] = acc
    q_g_copies = [
        remote(q_five.at[own_y], q_five.at[own_y], q_ss.at[base_g + o], q_rs.at[base_g + o], at_y(o))
        for o in offs_y
    ]
    for copy in q_g_copies:
        copy.start()

    in_copies[6].wait()
    in_copies[7].wait()
    moment = beta_one * mom[...] + (1.0 - beta_one) * grad
    second = beta_two * sec[...] + (1.0 - beta_two) * grad * grad
    update = learn_rate * (moment / first_fix) / (jnp.sqrt(second / second_fix) + adam_eps)
    free_n[...] = jnp.where(touched, fre[...] - update, fre[...])
    mom_n[...] = jnp.where(touched, moment, mom[...])
    sec_n[...] = jnp.where(touched, second, sec[...])
    out_copies = [
        pltpu.make_async_copy(src, dst, out_sem.at[i])
        for i, (src, dst) in enumerate(((free_n, free_o), (mom_n, mom_o), (sec_n, sec_o)))
    ]
    for copy in out_copies:
        copy.start()

    for p in range(pieces):
        acc = u_one[p, :, x]
        for copy, o in zip(u_x_copies[p], offs_x):
            copy.wait_recv()
            acc += u_x_in[p, o]
        for i in range(per_piece):
            w_two[1, p * per_piece + i] = acc[i]
            across_y(1, p * per_piece + i)

    for copy in q_g_copies:
        copy.wait_recv()
    q_back = remote(q_five, q_six, q_ss.at[base_g], q_rs.at[base_g], at_core)
    q_back.start()

    holder = y // per_core == c

    def last(k):
        @pl.when(jnp.logical_not(holder))
        def _():
            remote(
                w_two.at[k, 0, pl.ds(0, slice_rows)], w_y_in.at[k, 0], w_ss.at[k, 0, 0], w_rs.at[k, 0], at_core
            ).wait_recv()

        for o in offs_y:
            remote(
                w_two.at[k, 0, pl.ds(0, slice_rows)], w_y_in.at[k, o], w_ss.at[k, 0, 0], w_rs.at[k, o], at_y(o)
            ).wait_recv()
        acc = w_y_in[k, 0]
        for o in range(1, ny):
            acc += w_y_in[k, o]
        shift = rows_out - step_rows
        w_out[k] = jnp.where(c == 0, acc[:rows_out], acc[shift : shift + rows_out])
        pltpu.make_async_copy(w_out.at[k], (down_o, up_o)[k], out_sem.at[5 + k]).start()

    last(0)

    for half in range(2):
        cols = slice(half * (width // 2), (half + 1) * (width // 2))

        @pl.when(c == half)
        def _():
            pltpu.make_async_copy(q_five, query_o.at[:, cols], out_sem.at[3]).start()

    q_back.wait_recv()
    for half in range(2):
        cols = slice(half * (width // 2), (half + 1) * (width // 2))

        @pl.when(other == half)
        def _():
            pltpu.make_async_copy(q_six, query_o.at[:, cols], out_sem.at[4]).start()

    last(1)

    for o in offs_z:
        remote(enc.at[o], enc_in.at[o], enc_ss.at[o], enc_rs.at[o], at_z(o)).wait_send()
    for copy in (
        lv_copies + cnt_copies + score_copies + pool_copies + pool_back + lgr_copies + lga_copies
        + q_y_copies + q_x_copies + q_g_copies + og_copies + u_core + u_x_copies[0] + u_x_copies[1]
        + [q_core, q_back, og_core]
    ):
        copy.wait_send()
    for k in range(2):
        for b in range(per_core):
            o, copies = w_y_copies(k, b)
            copies[1].wait_send()

            @pl.when(o != 0)
            def _():
                copies[0].wait_send()

    for copy in out_copies:
        copy.wait()
    pltpu.make_async_copy(w_out.at[0], down_o, out_sem.at[5]).wait()
    pltpu.make_async_copy(w_out.at[1], up_o, out_sem.at[6]).wait()
    pltpu.make_async_copy(q_five, query_o.at[:, 0 : width // 2], out_sem.at[3]).wait()
    pltpu.make_async_copy(q_six, query_o.at[:, 0 : width // 2], out_sem.at[4]).wait()


def body(dims, queries, label_ids, label_text, up_weight, down_weight, free_vectors, moments, seconds):
    ny, nx, nc, nz = dims
    labels, tokens, width = label_text.shape
    units = up_weight.shape[1]
    rows = labels * tokens
    text_rows = label_text.reshape(rows, width)
    lz = labels // nz
    rows_out = width // (ny * nx * nc)
    chip_rows = rows_out * nc
    per_core = ny // nc
    half = width // 2
    qy = 192 // ny
    pieces = 2 if per_core % 2 == 0 else 1
    per_piece = per_core // pieces
    staged = -(-rows_out // 8) * 8
    vmem = pltpu.VMEM
    dma = pltpu.SemaphoreType.DMA
    scratch = [
        vmem((rows, width), BF16),
        vmem((width, rows), BF16),
        vmem((width, units), BF16),
        vmem((width, units), BF16),
        vmem((256, width), BF16),
        vmem((10, 192), jnp.int32),
        vmem((labels, width), F32),
        vmem((labels, width), F32),
        vmem((labels, width), F32),
        vmem((rows, units), F32),
        vmem((nx, nc, labels, units), F32),
        vmem((nx, 2 * nc * labels, units), BF16),
        vmem((nz, lz, width), F32),
        vmem((nz, lz, width), F32),
        vmem((labels, width), F32),
        vmem((labels, width), BF16),
        vmem((16, 128), F32),
        vmem((16, 128), F32),
        vmem((16, 128), F32),
        vmem((8, 128), F32),
        vmem((nz, 8, 128), F32),
        vmem((16, 128), F32),
        vmem((16, 128), F32),
        vmem((16, 128), F32),
        vmem((2, 16, 128), F32),
        vmem((nx, 16, 128), F32),
        vmem((ny, 16, 128), F32),
        vmem((labels, width), F32),
        vmem((nz, lz, width), F32),
        vmem((labels, width), F32),
        vmem((2, 192, half), F32),
        vmem((192, half), F32),
        vmem((192, half), F32),
        vmem((ny, qy, half), F32),
        vmem((nx, qy, half), F32),
        vmem((192, half), F32),
        vmem((192, half), F32),
        vmem((nc, labels, half), F32),
        vmem((per_core, nx, chip_rows, nc * labels), F32),
        vmem((nx, per_core, chip_rows, nc * labels), F32),
        vmem((rows, units), BF16),
        vmem((nc, pieces, per_piece, nx, chip_rows, units), F32),
        vmem((pieces, per_piece, nx, chip_rows, units), F32),
        vmem((pieces, per_piece, nx, chip_rows, units), F32),
        vmem((pieces, nx, per_piece, chip_rows, units), F32),
        vmem((2, per_core, chip_rows, units), F32),
        vmem((2, ny, staged, units), F32),
        vmem((2, rows_out, units), F32),
        vmem((labels, width), F32),
        vmem((labels, width), F32),
        vmem((labels, width), F32),
        dma((8,)),
        dma((nz,)),
        dma((7,)),
        dma((nz,)),
        dma((nz,)),
        dma((nz,)),
        dma((nz,)),
        dma((nz,)),
        dma((nz,)),
        dma((2 + nx + ny,)),
        dma((2 + nx + ny,)),
        dma((nz,)),
        dma((nz,)),
        dma((nz,)),
        dma((nz,)),
        dma((1 + nx + 2 * ny,)),
        dma((1 + nx + 2 * ny,)),
        dma((2 * nx,)),
        dma((2 * nx,)),
        dma((1 + nx,)),
        dma((1 + nx,)),
        dma((pieces, 1 + nx)),
        dma((pieces, 1 + nx)),
        dma((2, 2, per_core)),
        dma((2, ny)),
    ]
    hbm = pl.BlockSpec(memory_space=pl.ANY)
    flops = 2 * rows * width * units * 2
    results = pl.pallas_call(
        functools.partial(kernel, dims),
        out_shape=[
            jax.ShapeDtypeStruct((labels, width), F32),
            jax.ShapeDtypeStruct((labels, width), F32),
            jax.ShapeDtypeStruct((labels, width), F32),
            jax.ShapeDtypeStruct((192, width), F32),
            jax.ShapeDtypeStruct((rows_out, units), F32),
            jax.ShapeDtypeStruct((rows_out, units), F32),
        ],
        in_specs=[hbm] * 8,
        out_specs=[hbm] * 6,
        scratch_shapes=scratch,
        name="step",
        cost_estimate=pl.CostEstimate(flops=flops, bytes_accessed=8 * 2**20, transcendentals=rows * units),
        compiler_params=pltpu.CompilerParams(
            collective_id=0, has_side_effects=True, vmem_limit_bytes=56 * 2**20
        ),
    )(queries, label_ids.T, text_rows, up_weight, down_weight, free_vectors, moments, seconds)
    count = len(results)
    return pl.pallas_call(
        hand_over,
        out_shape=[jax.ShapeDtypeStruct(r.shape, r.dtype) for r in results],
        in_specs=[hbm] * count,
        out_specs=[hbm] * count,
        scratch_shapes=[vmem(r.shape, r.dtype) for r in results] + [dma((count,)), dma((count,))],
        name="hand_over",
    )(*results)


def hand_over(*refs):
    count = (len(refs) - 2) // 3
    loads = [pltpu.make_async_copy(refs[i], refs[2 * count + i], refs[-2].at[i]) for i in range(count)]
    stores = [
        pltpu.make_async_copy(refs[2 * count + i], refs[count + i], refs[-1].at[i]) for i in range(count)
    ]
    for copy in loads:
        copy.start()
    for load, store in zip(loads, stores):
        load.wait()
        store.start()
    for copy in stores:
        copy.wait()


def build(mesh, dims):
    placed = (
        P("query", None),
        P("query", None),
        P("label", None, None),
        P(None, "query"),
        P(None, "query"),
        P("label", None),
        P("label", None),
        P("label", None),
    )
    return jax.shard_map(
        functools.partial(body, dims),
        mesh=mesh,
        in_specs=placed,
        out_specs=(
            P("label", None),
            P("label", None),
            P("label", None),
            P("query", None),
            P("label", "query"),
            P("label", "query"),
        ),
        check_vma=False,
    )


def solution(mesh):
    return build(mesh, (8, 4, 2, mesh.shape["query"]))
```

```python
import functools
import math

import jax
import jax.numpy as jnp
from jax import lax
from jax.experimental import pallas as pl
from jax.experimental.pallas import tpu as pltpu
from jax.sharding import PartitionSpec as P

MESH = pl.DeviceIdType.MESH
F32 = jnp.float32
BF16 = jnp.bfloat16

beta_one = 0.9
beta_two = 0.999
adam_eps = 1e-08
learn_rate = 0.05
first_fix = 1.0 - 0.9**10
second_fix = 1.0 - 0.999**10
ROOT = math.sqrt(2.0 / math.pi)
CUBIC = 0.044715

NT = (((1,), (1,)), ((), ()))
TN = (((0,), (0,)), ((), ()))


def far_first(count):
    return sorted(range(1, count), key=lambda o: (-min(o, count - o), o))


def kernel(
    dims,
    queries_h,
    ids_h,
    text_h,
    up_h,
    down_h,
    free_h,
    mom_h,
    sec_h,
    free_o,
    mom_o,
    sec_o,
    query_o,
    up_o,
    down_o,
    text,
    text_t,
    upw,
    dnw,
    qp,
    ids,
    fre,
    mom,
    sec,
    slope,
    pool_in,
    pool_bf,
    enc,
    enc_in,
    lvec,
    lbf,
    idp,
    idt,
    idpack,
    cnt,
    cnt_in,
    sc_c,
    sc_x,
    sc_y,
    sc_c_in,
    sc_x_in,
    sc_y_in,
    lg_part,
    lg_in,
    lg,
    qt,
    q_c_in,
    q_one,
    q_x_in,
    q_two,
    q_y_in,
    q_four,
    q_five,
    q_six,
    lg_pair,
    og_t,
    og_in,
    pgrad,
    upart,
    u_c_in,
    u_one,
    u_x_in,
    w_two,
    w_y_in,
    w_out,
    free_n,
    mom_n,
    sec_n,
    in_sem,
    text_sem,
    out_sem,
    enc_ss,
    enc_rs,
    lv_ss,
    lv_rs,
    cnt_ss,
    cnt_rs,
    sc_ss,
    sc_rs,
    lgr_ss,
    lgr_rs,
    lga_ss,
    lga_rs,
    q_ss,
    q_rs,
    pool_ss,
    pool_rs,
    og_ss,
    og_rs,
    u_ss,
    u_rs,
    w_ss,
    w_rs,
):
    ny, nx, nc, nz = dims
    lab = lax.axis_index("label")
    z = lax.axis_index("query")
    y = lab // (nx * nc)
    x = (lab // nc) % nx
    c = lab % nc
    other = 1 - c
    offs_z, offs_y, offs_x = far_first(nz), far_first(ny), far_first(nx)
    labels, width = lvec.shape
    units = upw.shape[1]
    tokens = text.shape[0] // labels
    lz = labels // nz
    rows_z = text.shape[0] // nz

    def at_z(o):
        return (lab, (z + o) % nz)

    def at_y(o):
        return (((y + o) % ny * nx + x) * nc + c, z)

    def at_x(o):
        return ((y * nx + (x + o) % nx) * nc + c, z)

    def at_y_other(o):
        return (((y + o) % ny * nx + x) * nc + other, z)

    at_core = ((y * nx + x) * nc + other, z)

    barrier = pltpu.get_barrier_semaphore()
    peers = (
        [at_z(o) for o in offs_z]
        + [at_y(o) for o in offs_y]
        + [at_y_other(o) for o in offs_y]
        + [at_x(o) for o in offs_x]
        + [at_core]
    )
    for peer in peers:
        pl.semaphore_signal(barrier, inc=1, device_id=peer, device_id_type=MESH)

    def remote(src, dst, ss, rs, peer):
        return pltpu.make_async_remote_copy(
            src_ref=src,
            dst_ref=dst,
            send_sem=ss,
            recv_sem=rs,
            device_id=peer,
            device_id_type=MESH,
        )

    def offset_of(t):
        return (nz // 2 + (1 - 2 * (t % 2)) * ((t + 1) // 2)) % nz

    def text_copy(t):
        j = (z + offset_of(t)) % nz
        rows = pl.ds(pl.multiple_of(j * rows_z, rows_z), rows_z)
        return pltpu.make_async_copy(text_h.at[rows], text.at[rows], text_sem.at[t])

    in_copies = [
        pltpu.make_async_copy(src, dst, in_sem.at[i])
        for i, (src, dst) in enumerate(
            (
                (up_h, upw),
                (down_h, dnw),
                (free_h, fre),
                (ids_h, ids),
                (queries_h, qp.at[pl.ds(0, 192)]),
                (queries_h.at[pl.ds(128, 64)], qp.at[pl.ds(192, 64)]),
                (mom_h, mom),
                (sec_h, sec),
            )
        )
    ]
    in_copies[0].start()
    text_copy(0).start()
    in_copies[1].start()

    def start_text(t, carry):
        text_copy(t).start()
        return carry

    lax.fori_loop(1, nz, start_text, 0)
    for copy in in_copies[2:]:
        copy.start()
    in_copies[0].wait()

    def encode(t):
        o = offset_of(t)
        j = (z + o) % nz
        text_copy(t).wait()
        hidden = []
        for half in range(2):
            rows = pl.ds(pl.multiple_of(j * rows_z + half * (rows_z // 2), rows_z // 2), rows_z // 2)
            pre = jnp.dot(text[rows, :], upw[...], preferred_element_type=F32)
            square = pre * pre
            bent = jnp.tanh(pre * (ROOT + (ROOT * CUBIC) * square))
            gate = 0.5 + 0.5 * bent
            hidden.append(pre * gate)
            slope[rows, :] = gate + (0.5 * pre) * (1.0 - bent * bent) * (
                ROOT + (3.0 * ROOT * CUBIC) * square
            )
        hidden = jnp.concatenate(hidden, axis=0)
        mean = jnp.sum(hidden.reshape(lz, tokens, units), axis=1) * (1.0 / tokens)
        pool_in[0, c, pl.ds(pl.multiple_of(j * lz, lz), lz), :] = mean
        rest = mean - mean.astype(BF16).astype(F32)
        both = jnp.concatenate([mean, rest], axis=0).astype(BF16)
        out = lax.dot_general(both, dnw[...], NT, preferred_element_type=F32)
        enc[o] = out[:lz] + out[lz:]

    def enc_copy(t):
        o = offset_of(t)
        return remote(enc.at[o], enc_in.at[o], enc_ss.at[o], enc_rs.at[o], at_z(o))

    def encode_step(t, carry):
        encode(t)
        return carry

    def send_step(t, carry):
        enc_copy(t).start()
        return carry

    def encode_send_step(t, carry):
        encode(t)
        enc_copy(t).start()
        return carry

    early = min(2, nz - 1)
    in_copies[1].wait()
    lax.fori_loop(0, early, encode_step, 0)
    pl.semaphore_wait(barrier, len(peers))
    lax.fori_loop(0, early, send_step, 0)
    lax.fori_loop(early, nz - 1, encode_send_step, 0)
    encode(nz - 1)
    own_text = pl.ds(pl.multiple_of(z * rows_z, rows_z), rows_z)
    own_rows = pl.ds(pl.multiple_of(z * lz, lz), lz)
    text_mean = jnp.sum(text[own_text, :].astype(F32).reshape(lz, tokens, width), axis=1) * (1.0 / tokens)
    in_copies[2].wait()
    total = enc[0] + text_mean + fre[own_rows, :]
    for o in offs_z:
        remote(enc.at[o], enc_in.at[o], enc_ss.at[o], enc_rs.at[o], at_z(o)).wait_recv()
        total += enc_in[o]
    lvec[own_rows, :] = total
    lv_copies = [
        remote(lvec.at[own_rows], lvec.at[own_rows], lv_ss.at[o], lv_rs.at[o], at_z(o)) for o in offs_z
    ]
    for copy in lv_copies:
        copy.start()
    pool_copies = [remote(pool_in.at[0, c], pool_in.at[0, c], pool_ss.at[0], pool_rs.at[0], at_core)]
    pool_copies += [
        remote(pool_in.at[0, c], pool_in.at[o, c], pool_ss.at[o], pool_rs.at[o], at_x(o)) for o in offs_x
    ]
    for copy in pool_copies:
        copy.start()

    in_copies[3].wait()
    local = (ids[...] - lab * labels).astype(F32)
    idp[...] = jnp.full(idp.shape, -1.0, F32)
    idp[0:10, 0:64] = local[:, 128:192]
    idt[...] = pltpu.roll(idp[...], 64, 1)
    lane = lax.broadcasted_iota(jnp.int32, (1, 128), 1)
    idpack[...] = jnp.full(idpack.shape, -1.0, F32)
    idpack[0:10, :] = local[:, 0:128]
    for r in range(5):
        idpack[10 + r : 11 + r, :] = jnp.where(lane < 64, idp[r : r + 1, :], idt[r + 5 : r + 6, :])

    def owned(p, count):
        slots = lax.broadcasted_iota(jnp.int32, (count, 128), 0).astype(F32)
        return idpack[p : p + 1, :] == slots

    def packed(rows):
        acc = jnp.zeros((128, 128), F32)
        for p in rows:
            acc += jnp.where(owned(p, 128), 1.0, 0.0)
        return acc.astype(BF16)

    ones = jnp.ones((8, 128), BF16)
    cnt[...] = lax.dot_general(ones, packed(range(10)), NT, preferred_element_type=F32) + lax.dot_general(
        ones, packed(range(10, 15)), NT, preferred_element_type=F32
    )
    cnt_copies = [remote(cnt, cnt_in.at[o], cnt_ss.at[o], cnt_rs.at[o], at_z(o)) for o in offs_z]
    for copy in cnt_copies:
        copy.start()

    def turn(t, carry):
        rows = pl.ds(pl.multiple_of(t * 256, 256), 256)
        text_t[:, rows] = jnp.transpose(text[rows, :])
        return carry

    turns = text.shape[0] // 256
    in_copies[4].wait()
    in_copies[5].wait()

    lax.fori_loop(0, turns * 3 // 8, turn, 0)
    for copy in lv_copies:
        copy.wait_recv()
    lbf[...] = lvec[...].astype(BF16)

    similar = lax.dot_general(lbf[...], qp[...], NT, preferred_element_type=F32)
    sc_c[...] = jnp.zeros(sc_c.shape, F32)
    for p in range(15):
        block = similar[:, 0:128] if p < 10 else similar[:, 128:256]
        sc_c[p : p + 1, :] = jnp.sum(jnp.where(owned(p, labels), block, 0.0), axis=0, keepdims=True)
    score_copies = []

    def exchange(src, dst, base, offs, at, first, last):
        copies = [
            remote(src, dst.at[o], sc_ss.at[base + o], sc_rs.at[base + o], at(o)) for o in offs
        ]
        score_copies.extend(copies)
        for copy in copies:
            copy.start()
        lax.fori_loop(first, last, turn, 0)
        acc = src[...]
        for copy, o in zip(copies, offs):
            copy.wait_recv()
            acc += dst[o]
        return acc

    sc_x[...] = exchange(sc_c, sc_c_in, 0, [1], lambda o: at_core, 0, 0)
    sc_y[...] = exchange(sc_x, sc_x_in, 2, offs_x, at_x, turns * 3 // 8, turns * 5 // 8)
    scores = exchange(sc_y, sc_y_in, 2 + nx, offs_y, at_y, turns * 5 // 8, turns)

    temper = 1.0 / math.sqrt(width)
    scores = scores * temper
    top, low = scores[0:10], scores[10:15]
    top_max = jnp.max(top, axis=0, keepdims=True)
    low_max = jnp.max(low, axis=0, keepdims=True)
    low_max = jnp.maximum(low_max, pltpu.roll(low_max, 64, 1))
    top = jnp.exp(top - top_max)
    low = jnp.exp(low - low_max)
    top_sum = jnp.sum(top, axis=0, keepdims=True)
    low_sum = jnp.sum(low, axis=0, keepdims=True)
    low_sum = low_sum + pltpu.roll(low_sum, 64, 1)
    row_t = lax.broadcasted_iota(jnp.int32, (10, 128), 0)
    row_l = lax.broadcasted_iota(jnp.int32, (5, 128), 0)
    lane_l = lax.broadcasted_iota(jnp.int32, (5, 128), 1)
    top = (top / top_sum - jnp.where(row_t < 2, 0.5, 0.0)) * temper
    low = (low / low_sum - jnp.where((row_l < 2) & (lane_l < 64), 0.5, 0.0)) * temper
    top = top.astype(BF16).astype(F32)
    low = low.astype(BF16).astype(F32)
    spread = []
    for coef, base in ((top, 0), (low, 10)):
        acc = jnp.zeros((labels, 128), F32)
        for k in range(coef.shape[0]):
            acc += jnp.where(owned(base + k, labels), coef[k : k + 1], 0.0)
        spread.append(acc)
    spread = jnp.concatenate(spread, axis=1).astype(BF16)

    lg_part[...] = jnp.dot(spread, qp[...], preferred_element_type=F32)
    lgr_copies = []
    for o in offs_z:
        rows = pl.ds(pl.multiple_of((z + o) % nz * lz, lz), lz)
        lgr_copies.append(remote(lg_part.at[rows], lg_in.at[o], lgr_ss.at[o], lgr_rs.at[o], at_z(o)))
        lgr_copies[-1].start()

    terms = lax.dot_general(spread, lbf[...], TN, preferred_element_type=F32)
    for half in range(2):
        cols = slice(half * (width // 2), (half + 1) * (width // 2))
        qt[half, 0:128, :] = terms[0:128, cols]
        qt[half, 128:192, :] = terms[128:192, cols] + terms[192:256, cols]
    q_core = remote(qt.at[other], q_c_in, q_ss.at[0], q_rs.at[0], at_core)
    q_core.start()
    pool_back = []
    for copy, o in zip(pool_copies[1:], offs_x):
        copy.wait_recv()
        pool_back.append(
            remote(pool_in.at[o, c], pool_in.at[o, c], pool_ss.at[nx + o], pool_rs.at[nx + o], at_core)
        )
        pool_back[-1].start()
    qx = 192 // nx
    owners = 6 if ny == 8 else ny
    qy = qx // owners
    base_y, base_g, base_h = 1 + nx, 1 + nx + ny, 1 + nx + 2 * ny
    q_core.wait_recv()
    q_one[...] = qt[c] + q_c_in[...]
    q_x_copies = []
    for o in offs_x:
        rows = pl.ds(pl.multiple_of((x + o) % nx * qx, qx), qx)
        q_x_copies.append(remote(q_one.at[rows], q_x_in.at[o], q_ss.at[1 + o], q_rs.at[1 + o], at_x(o)))
        q_x_copies[-1].start()

    total = lg_part[own_rows, :]
    for copy, o in zip(lgr_copies, offs_z):
        copy.wait_recv()
        total += lg_in[o]
    lg[own_rows, :] = total
    lga_copies = [remote(lg.at[own_rows], lg.at[own_rows], lga_ss.at[o], lga_rs.at[o], at_z(o)) for o in offs_z]
    for copy in lga_copies:
        copy.start()

    seen = cnt[...]
    for copy, o in zip(cnt_copies, offs_z):
        copy.wait_recv()
        seen += cnt_in[o]
    diag = lax.broadcasted_iota(jnp.int32, (labels, 128), 0) == lax.broadcasted_iota(
        jnp.int32, (labels, 128), 1
    )
    touched = jnp.sum(jnp.where(diag, seen[0:1], 0.0), axis=1, keepdims=True) > 0.5

    own_x = pl.ds(pl.multiple_of(x * qx, qx), qx)
    acc = q_one[own_x, :]
    for copy, o in zip(q_x_copies, offs_x):
        copy.wait_recv()
        acc += q_x_in[o]
    q_two[...] = acc

    def q_y_copy(b):
        o = (b - y + ny) % ny
        return o, remote(
            q_two.at[pl.ds(b * qy, qy)],
            q_y_in.at[o],
            q_ss.at[base_y + b],
            q_rs.at[base_y + o],
            ((b * nx + x) * nc + c, z),
        )

    for b in range(owners):
        o, q_copy = q_y_copy(b)

        @pl.when(o != 0)
        def _():
            q_copy.start()

    pool_copies[0].wait_recv()
    for copy in pool_back:
        copy.wait_recv()
    for o in range(nx):
        for k in range(nc):
            mean = pool_in[o, k]
            whole = mean.astype(BF16)
            pool_bf[o, k * labels : (k + 1) * labels, :] = whole
            pool_bf[o, (nc + k) * labels : (nc + k + 1) * labels, :] = (mean - whole.astype(F32)).astype(BF16)

    for copy in lga_copies:
        copy.wait_recv()
    grad = lg[...]
    out_grad = grad.astype(BF16)
    hidden_grad = jnp.dot(out_grad, dnw[...], preferred_element_type=F32) * (1.0 / tokens)

    half_rows = width // nc
    cols_other = pl.ds(pl.multiple_of(other * half_rows, half_rows), half_rows)
    og_core = remote(lg.at[:, cols_other], lg_pair.at[c], og_ss.at[0], og_rs.at[0], at_core)
    og_core.start()

    lg_pair[c] = jnp.where(c == 0, grad[:, :half_rows], grad[:, half_rows:])
    for j in range(nz):
        rows = slice(j * rows_z, (j + 1) * rows_z)
        spreaded = jnp.broadcast_to(
            hidden_grad[j * lz : (j + 1) * lz, None, :], (lz, tokens, units)
        ).reshape(rows_z, units)
        pgrad[rows, :] = (slope[rows, :] * spreaded).astype(BF16)

    og_core.wait_recv()
    pair = lg_pair[...].reshape(nc * labels, half_rows).astype(BF16).astype(F32)
    og_t[...] = jnp.transpose(pair).reshape(og_t.shape)
    og_copies = []
    for o in offs_x:
        og_copies.append(
            remote(og_t.at[:, (x + o) % nx], og_in.at[o], og_ss.at[1 + o], og_rs.at[1 + o], at_x(o))
        )
        og_copies[-1].start()

    mine = pl.ds(pl.multiple_of(y % owners * qy, qy), qy)
    q_g_copies = [
        remote(q_four.at[mine], q_four.at[mine], q_ss.at[base_g + o], q_rs.at[base_g + y], at_y(o))
        for o in offs_y
    ]

    @pl.when(y < owners)
    def _():
        acc = q_two[mine, :]
        for o in offs_y:
            remote(
                q_two.at[pl.ds(0, qy)], q_y_in.at[o], q_ss.at[base_y], q_rs.at[base_y + o], at_y(o)
            ).wait_recv()
            acc += q_y_in[o]
        q_four[mine, :] = acc
        for copy in q_g_copies:
            copy.start()

    per_core = ny // nc
    pieces = 2 if per_core % 2 == 0 else 1
    per_piece = per_core // pieces
    piece_rows = half_rows // pieces

    def up_piece(h, p):
        rows = pl.ds(pl.multiple_of(h * half_rows + p * piece_rows, piece_rows), piece_rows)
        part = jnp.dot(text_t[rows, :], pgrad[...], preferred_element_type=F32)
        upart[h, p] = part.reshape(upart.shape[2:])

    u_core = []
    for p in range(pieces):
        up_piece(other, p)
        u_core.append(remote(upart.at[other, p], u_c_in.at[p], u_ss.at[p, 0], u_rs.at[p, 0], at_core))
        u_core[p].start()

    u_x_copies = [[], []]

    def across_x(p):
        u_core[p].wait_recv()
        u_one[p] = upart[c, p] + u_c_in[p]
        for o in offs_x:
            copy = remote(
                u_one.at[p, :, (x + o) % nx],
                u_x_in.at[p, o],
                u_ss.at[p, 1 + o],
                u_rs.at[p, 1 + o],
                at_x(o),
            )
            copy.start()
            u_x_copies[p].append(copy)

    for p in range(pieces):
        up_piece(c, p)
        across_x(p)

    rows_out = w_out.shape[1]
    step_rows, slice_rows = rows_out // 8 * 8, -(-rows_out // 8) * 8

    def w_y_copies(k, b):
        goal = c * per_core + b
        o = (goal - y + ny) % ny
        copies = []
        for side, core in enumerate((c, other)):
            rows = pl.ds(pl.multiple_of(core * step_rows, 8), slice_rows)
            copies.append(
                remote(
                    w_two.at[k, b, rows],
                    w_y_in.at[k, o],
                    w_ss.at[k, side, b],
                    w_rs.at[k, o],
                    ((goal * nx + x) * nc + core, z),
                )
            )
        return o, copies

    def across_y(k, b):
        o, copies = w_y_copies(k, b)
        copies[1].start()

        @pl.when(o != 0)
        def _():
            copies[0].start()

        @pl.when(o == 0)
        def _():
            w_y_in[k, 0] = w_two[k, b, pl.ds(pl.multiple_of(c * step_rows, 8), slice_rows), :]

    def down_term(values, o):
        values = values.reshape(half_rows // nx, nc * labels).astype(BF16)
        return jnp.dot(
            jnp.concatenate([values, values], axis=1), pool_bf[o], preferred_element_type=F32
        )

    acc = down_term(og_t[:, x], 0)
    for copy, o in zip(og_copies, offs_x):
        copy.wait_recv()
        acc += down_term(og_in[o], o)
    w_two[0] = acc.reshape(w_two.shape[1:])
    for b in range(per_core):
        across_y(0, b)

    for b in range(owners):

        @pl.when(y != b)
        def _():
            rows = pl.ds(b * qy, qy)
            remote(
                q_four.at[rows], q_four.at[rows], q_ss.at[base_g], q_rs.at[base_g + b], at_core
            ).wait_recv()

    q_five[own_x, :] = q_four[...]
    q_h_copies = [
        remote(q_four, q_five.at[own_x], q_ss.at[base_h + o], q_rs.at[base_h + o], at_x(o)) for o in offs_x
    ]
    for copy in q_h_copies:
        copy.start()

    in_copies[6].wait()
    in_copies[7].wait()
    moment = beta_one * mom[...] + (1.0 - beta_one) * grad
    second = beta_two * sec[...] + (1.0 - beta_two) * grad * grad
    update = learn_rate * (moment / first_fix) / (jnp.sqrt(second / second_fix) + adam_eps)
    free_n[...] = jnp.where(touched, fre[...] - update, fre[...])
    mom_n[...] = jnp.where(touched, moment, mom[...])
    sec_n[...] = jnp.where(touched, second, sec[...])
    out_copies = [
        pltpu.make_async_copy(src, dst, out_sem.at[i])
        for i, (src, dst) in enumerate(((free_n, free_o), (mom_n, mom_o), (sec_n, sec_o)))
    ]
    for copy in out_copies:
        copy.start()

    for p in range(pieces):
        acc = u_one[p, :, x]
        for copy, o in zip(u_x_copies[p], offs_x):
            copy.wait_recv()
            acc += u_x_in[p, o]
        for i in range(per_piece):
            w_two[1, p * per_piece + i] = acc[i]
            across_y(1, p * per_piece + i)

    for copy in q_h_copies:
        copy.wait_recv()
    q_back = remote(q_five, q_six, q_ss.at[base_h], q_rs.at[base_h], at_core)
    q_back.start()

    holder = y // per_core == c

    def last(k):
        @pl.when(jnp.logical_not(holder))
        def _():
            remote(
                w_two.at[k, 0, pl.ds(0, slice_rows)], w_y_in.at[k, 0], w_ss.at[k, 0, 0], w_rs.at[k, 0], at_core
            ).wait_recv()

        for o in offs_y:
            remote(
                w_two.at[k, 0, pl.ds(0, slice_rows)], w_y_in.at[k, o], w_ss.at[k, 0, 0], w_rs.at[k, o], at_y(o)
            ).wait_recv()
        acc = w_y_in[k, 0]
        for o in range(1, ny):
            acc += w_y_in[k, o]
        shift = rows_out - step_rows
        w_out[k] = jnp.where(c == 0, acc[:rows_out], acc[shift : shift + rows_out])
        pltpu.make_async_copy(w_out.at[k], (down_o, up_o)[k], out_sem.at[5 + k]).start()

    last(0)

    for half in range(2):
        cols = slice(half * (width // 2), (half + 1) * (width // 2))

        @pl.when(c == half)
        def _():
            pltpu.make_async_copy(q_five, query_o.at[:, cols], out_sem.at[3]).start()

    q_back.wait_recv()
    for half in range(2):
        cols = slice(half * (width // 2), (half + 1) * (width // 2))

        @pl.when(other == half)
        def _():
            pltpu.make_async_copy(q_six, query_o.at[:, cols], out_sem.at[4]).start()

    last(1)

    for o in offs_z:
        remote(enc.at[o], enc_in.at[o], enc_ss.at[o], enc_rs.at[o], at_z(o)).wait_send()
    for copy in (
        lv_copies + cnt_copies + score_copies + pool_copies + pool_back + lgr_copies + lga_copies
        + q_x_copies + q_h_copies + og_copies + u_core + u_x_copies[0] + u_x_copies[1]
        + [q_core, q_back, og_core]
    ):
        copy.wait_send()
    for b in range(owners):
        o, q_copy = q_y_copy(b)

        @pl.when(o != 0)
        def _():
            q_copy.wait_send()

    @pl.when(y < owners)
    def _():
        for copy in q_g_copies:
            copy.wait_send()

    for k in range(2):
        for b in range(per_core):
            o, copies = w_y_copies(k, b)
            copies[1].wait_send()

            @pl.when(o != 0)
            def _():
                copies[0].wait_send()

    for copy in out_copies:
        copy.wait()
    pltpu.make_async_copy(w_out.at[0], down_o, out_sem.at[5]).wait()
    pltpu.make_async_copy(w_out.at[1], up_o, out_sem.at[6]).wait()
    pltpu.make_async_copy(q_five, query_o.at[:, 0 : width // 2], out_sem.at[3]).wait()
    pltpu.make_async_copy(q_six, query_o.at[:, 0 : width // 2], out_sem.at[4]).wait()


def body(dims, queries, label_ids, label_text, up_weight, down_weight, free_vectors, moments, seconds):
    ny, nx, nc, nz = dims
    labels, tokens, width = label_text.shape
    units = up_weight.shape[1]
    rows = labels * tokens
    text_rows = label_text.reshape(rows, width)
    lz = labels // nz
    rows_out = width // (ny * nx * nc)
    chip_rows = rows_out * nc
    per_core = ny // nc
    half = width // 2
    qx = 192 // nx
    qy = qx // (6 if ny == 8 else ny)
    pieces = 2 if per_core % 2 == 0 else 1
    per_piece = per_core // pieces
    staged = -(-rows_out // 8) * 8
    vmem = pltpu.VMEM
    dma = pltpu.SemaphoreType.DMA
    scratch = [
        vmem((rows, width), BF16),
        vmem((width, rows), BF16),
        vmem((width, units), BF16),
        vmem((width, units), BF16),
        vmem((256, width), BF16),
        vmem((10, 192), jnp.int32),
        vmem((labels, width), F32),
        vmem((labels, width), F32),
        vmem((labels, width), F32),
        vmem((rows, units), F32),
        vmem((nx, nc, labels, units), F32),
        vmem((nx, 2 * nc * labels, units), BF16),
        vmem((nz, lz, width), F32),
        vmem((nz, lz, width), F32),
        vmem((labels, width), F32),
        vmem((labels, width), BF16),
        vmem((16, 128), F32),
        vmem((16, 128), F32),
        vmem((16, 128), F32),
        vmem((8, 128), F32),
        vmem((nz, 8, 128), F32),
        vmem((16, 128), F32),
        vmem((16, 128), F32),
        vmem((16, 128), F32),
        vmem((2, 16, 128), F32),
        vmem((nx, 16, 128), F32),
        vmem((ny, 16, 128), F32),
        vmem((labels, width), F32),
        vmem((nz, lz, width), F32),
        vmem((labels, width), F32),
        vmem((2, 192, half), F32),
        vmem((192, half), F32),
        vmem((192, half), F32),
        vmem((nx, qx, half), F32),
        vmem((qx, half), F32),
        vmem((ny, qy, half), F32),
        vmem((qx, half), F32),
        vmem((192, half), F32),
        vmem((192, half), F32),
        vmem((nc, labels, half), F32),
        vmem((per_core, nx, chip_rows, nc * labels), F32),
        vmem((nx, per_core, chip_rows, nc * labels), F32),
        vmem((rows, units), BF16),
        vmem((nc, pieces, per_piece, nx, chip_rows, units), F32),
        vmem((pieces, per_piece, nx, chip_rows, units), F32),
        vmem((pieces, per_piece, nx, chip_rows, units), F32),
        vmem((pieces, nx, per_piece, chip_rows, units), F32),
        vmem((2, per_core, chip_rows, units), F32),
        vmem((2, ny, staged, units), F32),
        vmem((2, rows_out, units), F32),
        vmem((labels, width), F32),
        vmem((labels, width), F32),
        vmem((labels, width), F32),
        dma((8,)),
        dma((nz,)),
        dma((7,)),
        dma((nz,)),
        dma((nz,)),
        dma((nz,)),
        dma((nz,)),
        dma((nz,)),
        dma((nz,)),
        dma((2 + nx + ny,)),
        dma((2 + nx + ny,)),
        dma((nz,)),
        dma((nz,)),
        dma((nz,)),
        dma((nz,)),
        dma((1 + 2 * nx + 2 * ny,)),
        dma((1 + 2 * nx + 2 * ny,)),
        dma((2 * nx,)),
        dma((2 * nx,)),
        dma((1 + nx,)),
        dma((1 + nx,)),
        dma((pieces, 1 + nx)),
        dma((pieces, 1 + nx)),
        dma((2, 2, per_core)),
        dma((2, ny)),
    ]
    hbm = pl.BlockSpec(memory_space=pl.ANY)
    flops = 2 * rows * width * units * 2
    results = pl.pallas_call(
        functools.partial(kernel, dims),
        out_shape=[
            jax.ShapeDtypeStruct((labels, width), F32),
            jax.ShapeDtypeStruct((labels, width), F32),
            jax.ShapeDtypeStruct((labels, width), F32),
            jax.ShapeDtypeStruct((192, width), F32),
            jax.ShapeDtypeStruct((rows_out, units), F32),
            jax.ShapeDtypeStruct((rows_out, units), F32),
        ],
        in_specs=[hbm] * 8,
        out_specs=[hbm] * 6,
        scratch_shapes=scratch,
        name="step",
        cost_estimate=pl.CostEstimate(flops=flops, bytes_accessed=8 * 2**20, transcendentals=rows * units),
        compiler_params=pltpu.CompilerParams(
            collective_id=0, has_side_effects=True, vmem_limit_bytes=56 * 2**20
        ),
    )(queries, label_ids.T, text_rows, up_weight, down_weight, free_vectors, moments, seconds)
    count = len(results)
    return pl.pallas_call(
        hand_over,
        out_shape=[jax.ShapeDtypeStruct(r.shape, r.dtype) for r in results],
        in_specs=[hbm] * count,
        out_specs=[hbm] * count,
        scratch_shapes=[vmem(r.shape, r.dtype) for r in results] + [dma((count,)), dma((count,))],
        name="hand_over",
    )(*results)


def hand_over(*refs):
    count = (len(refs) - 2) // 3
    loads = [pltpu.make_async_copy(refs[i], refs[2 * count + i], refs[-2].at[i]) for i in range(count)]
    stores = [
        pltpu.make_async_copy(refs[2 * count + i], refs[count + i], refs[-1].at[i]) for i in range(count)
    ]
    for copy in loads:
        copy.start()
    for load, store in zip(loads, stores):
        load.wait()
        store.start()
    for copy in stores:
        copy.wait()


def build(mesh, dims):
    placed = (
        P("query", None),
        P("query", None),
        P("label", None, None),
        P(None, "query"),
        P(None, "query"),
        P("label", None),
        P("label", None),
        P("label", None),
    )
    return jax.shard_map(
        functools.partial(body, dims),
        mesh=mesh,
        in_specs=placed,
        out_specs=(
            P("label", None),
            P("label", None),
            P("label", None),
            P("query", None),
            P("label", "query"),
            P("label", "query"),
        ),
        check_vma=False,
    )


def solution(mesh):
    return build(mesh, (8, 4, 2, mesh.shape["query"]))
```

```python
import functools
import math

import jax
import jax.numpy as jnp
from jax import lax
from jax.experimental import pallas as pl
from jax.experimental.pallas import tpu as pltpu
from jax.sharding import PartitionSpec as P

MESH = pl.DeviceIdType.MESH
F32 = jnp.float32
BF16 = jnp.bfloat16

beta_one = 0.9
beta_two = 0.999
adam_eps = 1e-08
learn_rate = 0.05
first_fix = 1.0 - 0.9**10
second_fix = 1.0 - 0.999**10
ROOT = math.sqrt(2.0 / math.pi)
CUBIC = 0.044715

NT = (((1,), (1,)), ((), ()))
TN = (((0,), (0,)), ((), ()))


def far_first(count):
    return sorted(range(1, count), key=lambda o: (-min(o, count - o), o))


def kernel(
    dims,
    queries_h,
    ids_h,
    text_h,
    up_h,
    down_h,
    free_h,
    mom_h,
    sec_h,
    free_o,
    mom_o,
    sec_o,
    query_o,
    up_o,
    down_o,
    text,
    text_t,
    upw,
    dnw,
    qp,
    ids,
    fre,
    mom,
    sec,
    slope,
    pool_in,
    pool_bf,
    enc,
    enc_in,
    lvec,
    lbf,
    idp,
    idt,
    idpack,
    cnt,
    cnt_in,
    sc_c,
    sc_x,
    sc_y,
    sc_c_in,
    sc_x_in,
    sc_y_in,
    lg_part,
    lg_in,
    lg,
    qt,
    q_c_in,
    q_one,
    q_x_in,
    q_two,
    q_y_in,
    q_four,
    q_five,
    q_six,
    lg_pair,
    og_t,
    og_in,
    pgrad,
    upart,
    u_c_in,
    u_one,
    u_x_in,
    w_two,
    w_y_in,
    w_out,
    free_n,
    mom_n,
    sec_n,
    in_sem,
    text_sem,
    out_sem,
    enc_ss,
    enc_rs,
    lv_ss,
    lv_rs,
    cnt_ss,
    cnt_rs,
    sc_ss,
    sc_rs,
    lgr_ss,
    lgr_rs,
    lga_ss,
    lga_rs,
    q_ss,
    q_rs,
    pool_ss,
    pool_rs,
    og_ss,
    og_rs,
    u_ss,
    u_rs,
    w_ss,
    w_rs,
):
    ny, nx, nc, nz = dims
    lab = lax.axis_index("label")
    z = lax.axis_index("query")
    y = lab // (nx * nc)
    x = (lab // nc) % nx
    c = lab % nc
    other = 1 - c
    offs_z, offs_y, offs_x = far_first(nz), far_first(ny), far_first(nx)
    labels, width = lvec.shape
    units = upw.shape[1]
    tokens = text.shape[0] // labels
    lz = labels // nz
    rows_z = text.shape[0] // nz

    def at_z(o):
        return (lab, (z + o) % nz)

    def at_y(o):
        return (((y + o) % ny * nx + x) * nc + c, z)

    def at_x(o):
        return ((y * nx + (x + o) % nx) * nc + c, z)

    def at_y_other(o):
        return (((y + o) % ny * nx + x) * nc + other, z)

    at_core = ((y * nx + x) * nc + other, z)

    barrier = pltpu.get_barrier_semaphore()
    peers = (
        [at_z(o) for o in offs_z]
        + [at_y(o) for o in offs_y]
        + [at_y_other(o) for o in offs_y]
        + [at_x(o) for o in offs_x]
        + [at_core]
    )
    for peer in peers:
        pl.semaphore_signal(barrier, inc=1, device_id=peer, device_id_type=MESH)

    def remote(src, dst, ss, rs, peer):
        return pltpu.make_async_remote_copy(
            src_ref=src,
            dst_ref=dst,
            send_sem=ss,
            recv_sem=rs,
            device_id=peer,
            device_id_type=MESH,
        )

    def offset_of(t):
        return (nz // 2 + (1 - 2 * (t % 2)) * ((t + 1) // 2)) % nz

    def text_copy(t):
        j = (z + offset_of(t)) % nz
        rows = pl.ds(pl.multiple_of(j * rows_z, rows_z), rows_z)
        return pltpu.make_async_copy(text_h.at[rows], text.at[rows], text_sem.at[t])

    in_copies = [
        pltpu.make_async_copy(src, dst, in_sem.at[i])
        for i, (src, dst) in enumerate(
            (
                (up_h, upw),
                (down_h, dnw),
                (free_h, fre),
                (ids_h, ids),
                (queries_h, qp.at[pl.ds(0, 192)]),
                (queries_h.at[pl.ds(128, 64)], qp.at[pl.ds(192, 64)]),
                (mom_h, mom),
                (sec_h, sec),
            )
        )
    ]
    in_copies[0].start()
    text_copy(0).start()
    in_copies[1].start()

    def start_text(t, carry):
        text_copy(t).start()
        return carry

    lax.fori_loop(1, nz, start_text, 0)
    for copy in in_copies[2:]:
        copy.start()
    in_copies[0].wait()

    def encode(t):
        o = offset_of(t)
        j = (z + o) % nz
        text_copy(t).wait()
        hidden = []
        for half in range(2):
            rows = pl.ds(pl.multiple_of(j * rows_z + half * (rows_z // 2), rows_z // 2), rows_z // 2)
            pre = jnp.dot(text[rows, :], upw[...], preferred_element_type=F32)
            square = pre * pre
            bent = jnp.tanh(pre * (ROOT + (ROOT * CUBIC) * square))
            gate = 0.5 + 0.5 * bent
            hidden.append(pre * gate)
            slope[rows, :] = gate + (0.5 * pre) * (1.0 - bent * bent) * (
                ROOT + (3.0 * ROOT * CUBIC) * square
            )
        hidden = jnp.concatenate(hidden, axis=0)
        mean = jnp.sum(hidden.reshape(lz, tokens, units), axis=1) * (1.0 / tokens)
        pool_in[0, c, pl.ds(pl.multiple_of(j * lz, lz), lz), :] = mean
        rest = mean - mean.astype(BF16).astype(F32)
        both = jnp.concatenate([mean, rest], axis=0).astype(BF16)
        out = lax.dot_general(both, dnw[...], NT, preferred_element_type=F32)
        enc[o] = out[:lz] + out[lz:]

    def enc_copy(t):
        o = offset_of(t)
        return remote(enc.at[o], enc_in.at[o], enc_ss.at[o], enc_rs.at[o], at_z(o))

    def encode_step(t, carry):
        encode(t)
        return carry

    def send_step(t, carry):
        enc_copy(t).start()
        return carry

    def encode_send_step(t, carry):
        encode(t)
        enc_copy(t).start()
        return carry

    early = min(2, nz - 1)
    in_copies[1].wait()
    lax.fori_loop(0, early, encode_step, 0)
    pl.semaphore_wait(barrier, len(peers))
    lax.fori_loop(0, early, send_step, 0)
    lax.fori_loop(early, nz - 1, encode_send_step, 0)
    encode(nz - 1)
    own_text = pl.ds(pl.multiple_of(z * rows_z, rows_z), rows_z)
    own_rows = pl.ds(pl.multiple_of(z * lz, lz), lz)
    text_mean = jnp.sum(text[own_text, :].astype(F32).reshape(lz, tokens, width), axis=1) * (1.0 / tokens)
    in_copies[2].wait()
    total = enc[0] + text_mean + fre[own_rows, :]
    for o in offs_z:
        remote(enc.at[o], enc_in.at[o], enc_ss.at[o], enc_rs.at[o], at_z(o)).wait_recv()
        total += enc_in[o]
    lvec[own_rows, :] = total
    lv_copies = [
        remote(lvec.at[own_rows], lvec.at[own_rows], lv_ss.at[o], lv_rs.at[o], at_z(o)) for o in offs_z
    ]
    for copy in lv_copies:
        copy.start()
    pool_copies = [remote(pool_in.at[0, c], pool_in.at[0, c], pool_ss.at[0], pool_rs.at[0], at_core)]
    pool_copies += [
        remote(pool_in.at[0, c], pool_in.at[o, c], pool_ss.at[o], pool_rs.at[o], at_x(o)) for o in offs_x
    ]
    for copy in pool_copies:
        copy.start()

    in_copies[3].wait()
    local = (ids[...] - lab * labels).astype(F32)
    idp[...] = jnp.full(idp.shape, -1.0, F32)
    idp[0:10, 0:64] = local[:, 128:192]
    idt[...] = pltpu.roll(idp[...], 64, 1)
    lane = lax.broadcasted_iota(jnp.int32, (1, 128), 1)
    idpack[...] = jnp.full(idpack.shape, -1.0, F32)
    idpack[0:10, :] = local[:, 0:128]
    for r in range(5):
        idpack[10 + r : 11 + r, :] = jnp.where(lane < 64, idp[r : r + 1, :], idt[r + 5 : r + 6, :])

    def owned(p, count):
        slots = lax.broadcasted_iota(jnp.int32, (count, 128), 0).astype(F32)
        return idpack[p : p + 1, :] == slots

    def packed(rows):
        acc = jnp.zeros((128, 128), F32)
        for p in rows:
            acc += jnp.where(owned(p, 128), 1.0, 0.0)
        return acc.astype(BF16)

    ones = jnp.ones((8, 128), BF16)
    cnt[...] = lax.dot_general(ones, packed(range(10)), NT, preferred_element_type=F32) + lax.dot_general(
        ones, packed(range(10, 15)), NT, preferred_element_type=F32
    )
    cnt_copies = [remote(cnt, cnt_in.at[o], cnt_ss.at[o], cnt_rs.at[o], at_z(o)) for o in offs_z]
    for copy in cnt_copies:
        copy.start()

    def turn(t, carry):
        rows = pl.ds(pl.multiple_of(t * 256, 256), 256)
        text_t[:, rows] = jnp.transpose(text[rows, :])
        return carry

    turns = text.shape[0] // 256
    in_copies[4].wait()
    in_copies[5].wait()

    lax.fori_loop(0, turns * 3 // 8, turn, 0)
    for copy in lv_copies:
        copy.wait_recv()
    lbf[...] = lvec[...].astype(BF16)

    similar = lax.dot_general(lbf[...], qp[...], NT, preferred_element_type=F32)
    sc_c[...] = jnp.zeros(sc_c.shape, F32)
    for p in range(15):
        block = similar[:, 0:128] if p < 10 else similar[:, 128:256]
        sc_c[p : p + 1, :] = jnp.sum(jnp.where(owned(p, labels), block, 0.0), axis=0, keepdims=True)
    score_copies = []

    def exchange(src, dst, base, offs, at, first, last):
        copies = [
            remote(src, dst.at[o], sc_ss.at[base + o], sc_rs.at[base + o], at(o)) for o in offs
        ]
        score_copies.extend(copies)
        for copy in copies:
            copy.start()
        lax.fori_loop(first, last, turn, 0)
        acc = src[...]
        for copy, o in zip(copies, offs):
            copy.wait_recv()
            acc += dst[o]
        return acc

    sc_x[...] = exchange(sc_c, sc_c_in, 0, [1], lambda o: at_core, 0, 0)
    sc_y[...] = exchange(sc_x, sc_x_in, 2, offs_x, at_x, turns * 3 // 8, turns * 5 // 8)
    scores = exchange(sc_y, sc_y_in, 2 + nx, offs_y, at_y, turns * 5 // 8, turns)

    temper = 1.0 / math.sqrt(width)
    scores = scores * temper
    top, low = scores[0:10], scores[10:15]
    top_max = jnp.max(top, axis=0, keepdims=True)
    low_max = jnp.max(low, axis=0, keepdims=True)
    low_max = jnp.maximum(low_max, pltpu.roll(low_max, 64, 1))
    top = jnp.exp(top - top_max)
    low = jnp.exp(low - low_max)
    top_sum = jnp.sum(top, axis=0, keepdims=True)
    low_sum = jnp.sum(low, axis=0, keepdims=True)
    low_sum = low_sum + pltpu.roll(low_sum, 64, 1)
    row_t = lax.broadcasted_iota(jnp.int32, (10, 128), 0)
    row_l = lax.broadcasted_iota(jnp.int32, (5, 128), 0)
    lane_l = lax.broadcasted_iota(jnp.int32, (5, 128), 1)
    top = (top / top_sum - jnp.where(row_t < 2, 0.5, 0.0)) * temper
    low = (low / low_sum - jnp.where((row_l < 2) & (lane_l < 64), 0.5, 0.0)) * temper
    top = top.astype(BF16).astype(F32)
    low = low.astype(BF16).astype(F32)
    spread = []
    for coef, base in ((top, 0), (low, 10)):
        acc = jnp.zeros((labels, 128), F32)
        for k in range(coef.shape[0]):
            acc += jnp.where(owned(base + k, labels), coef[k : k + 1], 0.0)
        spread.append(acc)
    spread = jnp.concatenate(spread, axis=1).astype(BF16)

    lg_part[...] = jnp.dot(spread, qp[...], preferred_element_type=F32)
    lgr_copies = []
    for o in offs_z:
        rows = pl.ds(pl.multiple_of((z + o) % nz * lz, lz), lz)
        lgr_copies.append(remote(lg_part.at[rows], lg_in.at[o], lgr_ss.at[o], lgr_rs.at[o], at_z(o)))
        lgr_copies[-1].start()

    terms = lax.dot_general(spread, lbf[...], TN, preferred_element_type=F32)
    for half in range(2):
        cols = slice(half * (width // 2), (half + 1) * (width // 2))
        qt[half, 0:128, :] = terms[0:128, cols]
        qt[half, 128:192, :] = terms[128:192, cols] + terms[192:256, cols]
    q_core = remote(qt.at[other], q_c_in, q_ss.at[0], q_rs.at[0], at_core)
    q_core.start()
    pool_back = []
    for copy, o in zip(pool_copies[1:], offs_x):
        copy.wait_recv()
        pool_back.append(
            remote(pool_in.at[o, c], pool_in.at[o, c], pool_ss.at[nx + o], pool_rs.at[nx + o], at_core)
        )
        pool_back[-1].start()
    qx = 192 // nx
    owners = 6 if ny == 8 else ny
    qy = qx // owners
    base_y, base_g, base_h = 1 + nx, 1 + nx + ny, 1 + nx + 2 * ny
    q_core.wait_recv()
    q_one[...] = qt[c] + q_c_in[...]
    q_x_copies = []
    for o in offs_x:
        rows = pl.ds(pl.multiple_of((x + o) % nx * qx, qx), qx)
        q_x_copies.append(remote(q_one.at[rows], q_x_in.at[o], q_ss.at[1 + o], q_rs.at[1 + o], at_x(o)))
        q_x_copies[-1].start()

    total = lg_part[own_rows, :]
    for copy, o in zip(lgr_copies, offs_z):
        copy.wait_recv()
        total += lg_in[o]
    lg[own_rows, :] = total
    lga_copies = [remote(lg.at[own_rows], lg.at[own_rows], lga_ss.at[o], lga_rs.at[o], at_z(o)) for o in offs_z]
    for copy in lga_copies:
        copy.start()

    seen = cnt[...]
    for copy, o in zip(cnt_copies, offs_z):
        copy.wait_recv()
        seen += cnt_in[o]
    diag = lax.broadcasted_iota(jnp.int32, (labels, 128), 0) == lax.broadcasted_iota(
        jnp.int32, (labels, 128), 1
    )
    touched = jnp.sum(jnp.where(diag, seen[0:1], 0.0), axis=1, keepdims=True) > 0.5

    own_x = pl.ds(pl.multiple_of(x * qx, qx), qx)
    acc = q_one[own_x, :]
    for copy, o in zip(q_x_copies, offs_x):
        copy.wait_recv()
        acc += q_x_in[o]
    q_two[...] = acc

    def q_y_copy(b):
        o = (b - y + ny) % ny
        return o, remote(
            q_two.at[pl.ds(b * qy, qy)],
            q_y_in.at[o],
            q_ss.at[base_y + b],
            q_rs.at[base_y + o],
            ((b * nx + x) * nc + c, z),
        )

    for b in range(owners):
        o, q_copy = q_y_copy(b)

        @pl.when(o != 0)
        def _():
            q_copy.start()

    pool_copies[0].wait_recv()
    for copy in pool_back:
        copy.wait_recv()
    for o in range(nx):
        for k in range(nc):
            mean = pool_in[o, k]
            whole = mean.astype(BF16)
            pool_bf[o, k * labels : (k + 1) * labels, :] = whole
            pool_bf[o, (nc + k) * labels : (nc + k + 1) * labels, :] = (mean - whole.astype(F32)).astype(BF16)

    for copy in lga_copies:
        copy.wait_recv()
    grad = lg[...]
    out_grad = grad.astype(BF16)
    hidden_grad = jnp.dot(out_grad, dnw[...], preferred_element_type=F32) * (1.0 / tokens)

    half_rows = width // nc
    cols_other = pl.ds(pl.multiple_of(other * half_rows, half_rows), half_rows)
    og_core = remote(lg.at[:, cols_other], lg_pair.at[c], og_ss.at[0], og_rs.at[0], at_core)
    og_core.start()

    lg_pair[c] = jnp.where(c == 0, grad[:, :half_rows], grad[:, half_rows:])
    for j in range(nz):
        rows = slice(j * rows_z, (j + 1) * rows_z)
        spreaded = jnp.broadcast_to(
            hidden_grad[j * lz : (j + 1) * lz, None, :], (lz, tokens, units)
        ).reshape(rows_z, units)
        pgrad[rows, :] = (slope[rows, :] * spreaded).astype(BF16)

    og_core.wait_recv()
    pair = lg_pair[...].reshape(nc * labels, half_rows).astype(BF16).astype(F32)
    og_t[...] = jnp.transpose(pair).reshape(og_t.shape)
    og_copies = []
    for o in offs_x:
        og_copies.append(
            remote(og_t.at[:, (x + o) % nx], og_in.at[o], og_ss.at[1 + o], og_rs.at[1 + o], at_x(o))
        )
        og_copies[-1].start()

    mine = pl.ds(pl.multiple_of(y % owners * qy, qy), qy)
    q_g_copies = [
        remote(q_four.at[mine], q_four.at[mine], q_ss.at[base_g + o], q_rs.at[base_g + y], at_y(o))
        for o in offs_y
    ]

    @pl.when(y < owners)
    def _():
        acc = q_two[mine, :]
        for o in offs_y:
            remote(
                q_two.at[pl.ds(0, qy)], q_y_in.at[o], q_ss.at[base_y], q_rs.at[base_y + o], at_y(o)
            ).wait_recv()
            acc += q_y_in[o]
        q_four[mine, :] = acc
        for copy in q_g_copies:
            copy.start()

    per_core = ny // nc
    pieces = 2 if per_core % 2 == 0 else 1
    per_piece = per_core // pieces
    piece_rows = half_rows // pieces

    def up_piece(h, p):
        rows = pl.ds(pl.multiple_of(h * half_rows + p * piece_rows, piece_rows), piece_rows)
        part = jnp.dot(text_t[rows, :], pgrad[...], preferred_element_type=F32)
        upart[h, p] = part.reshape(upart.shape[2:])

    u_core = []
    for p in range(pieces):
        up_piece(other, p)
        u_core.append(remote(upart.at[other, p], u_c_in.at[p], u_ss.at[p, 0], u_rs.at[p, 0], at_core))
        u_core[p].start()

    u_x_copies = [[], []]

    def across_x(p):
        u_core[p].wait_recv()
        u_one[p] = upart[c, p] + u_c_in[p]
        for o in offs_x:
            copy = remote(
                u_one.at[p, :, (x + o) % nx],
                u_x_in.at[p, o],
                u_ss.at[p, 1 + o],
                u_rs.at[p, 1 + o],
                at_x(o),
            )
            copy.start()
            u_x_copies[p].append(copy)

    for p in range(pieces):
        up_piece(c, p)
        across_x(p)

    rows_out = w_out.shape[1]
    step_rows, slice_rows = rows_out // 8 * 8, -(-rows_out // 8) * 8

    def w_y_copies(k, b):
        goal = c * per_core + b
        o = (goal - y + ny) % ny
        copies = []
        for side, core in enumerate((c, other)):
            rows = pl.ds(pl.multiple_of(core * step_rows, 8), slice_rows)
            copies.append(
                remote(
                    w_two.at[k, b, rows],
                    w_y_in.at[k, o],
                    w_ss.at[k, side, b],
                    w_rs.at[k, o],
                    ((goal * nx + x) * nc + core, z),
                )
            )
        return o, copies

    def across_y(k, b):
        o, copies = w_y_copies(k, b)
        copies[1].start()

        @pl.when(o != 0)
        def _():
            copies[0].start()

        @pl.when(o == 0)
        def _():
            w_y_in[k, 0] = w_two[k, b, pl.ds(pl.multiple_of(c * step_rows, 8), slice_rows), :]

    def down_term(values, o):
        values = values.reshape(half_rows // nx, nc * labels).astype(BF16)
        return jnp.dot(
            jnp.concatenate([values, values], axis=1), pool_bf[o], preferred_element_type=F32
        )

    acc = down_term(og_t[:, x], 0)
    for copy, o in zip(og_copies, offs_x):
        copy.wait_recv()
        acc += down_term(og_in[o], o)
    w_two[0] = acc.reshape(w_two.shape[1:])
    for b in range(per_core):
        across_y(0, b)

    for b in range(owners):

        @pl.when(y != b)
        def _():
            rows = pl.ds(b * qy, qy)
            remote(
                q_four.at[rows], q_four.at[rows], q_ss.at[base_g], q_rs.at[base_g + b], at_core
            ).wait_recv()

    q_five[own_x, :] = q_four[...]
    q_h_copies = [
        remote(q_four, q_five.at[own_x], q_ss.at[base_h + o], q_rs.at[base_h + o], at_x(o)) for o in offs_x
    ]
    for copy in q_h_copies:
        copy.start()

    in_copies[6].wait()
    in_copies[7].wait()
    moment = beta_one * mom[...] + (1.0 - beta_one) * grad
    second = beta_two * sec[...] + (1.0 - beta_two) * grad * grad
    update = learn_rate * (moment / first_fix) / (jnp.sqrt(second / second_fix) + adam_eps)
    free_n[...] = jnp.where(touched, fre[...] - update, fre[...])
    mom_n[...] = jnp.where(touched, moment, mom[...])
    sec_n[...] = jnp.where(touched, second, sec[...])
    out_copies = [
        pltpu.make_async_copy(src, dst, out_sem.at[i])
        for i, (src, dst) in enumerate(((free_n, free_o), (mom_n, mom_o), (sec_n, sec_o)))
    ]
    for copy in out_copies:
        copy.start()

    for p in range(pieces):
        acc = u_one[p, :, x]
        for copy, o in zip(u_x_copies[p], offs_x):
            copy.wait_recv()
            acc += u_x_in[p, o]
        for i in range(per_piece):
            w_two[1, p * per_piece + i] = acc[i]
            across_y(1, p * per_piece + i)

    for copy in q_h_copies:
        copy.wait_recv()
    q_back = remote(q_five, q_six, q_ss.at[base_h], q_rs.at[base_h], at_core)
    q_back.start()

    holder = y // per_core == c

    def last(k):
        @pl.when(jnp.logical_not(holder))
        def _():
            remote(
                w_two.at[k, 0, pl.ds(0, slice_rows)], w_y_in.at[k, 0], w_ss.at[k, 0, 0], w_rs.at[k, 0], at_core
            ).wait_recv()

        for o in offs_y:
            remote(
                w_two.at[k, 0, pl.ds(0, slice_rows)], w_y_in.at[k, o], w_ss.at[k, 0, 0], w_rs.at[k, o], at_y(o)
            ).wait_recv()
        acc = w_y_in[k, 0]
        for o in range(1, ny):
            acc += w_y_in[k, o]
        shift = rows_out - step_rows
        w_out[k] = jnp.where(c == 0, acc[:rows_out], acc[shift : shift + rows_out])
        pltpu.make_async_copy(w_out.at[k], (down_o, up_o)[k], out_sem.at[5 + k]).start()

    last(0)

    for half in range(2):
        cols = slice(half * (width // 2), (half + 1) * (width // 2))

        @pl.when(c == half)
        def _():
            pltpu.make_async_copy(q_five, query_o.at[:, cols], out_sem.at[3]).start()

    q_back.wait_recv()
    for half in range(2):
        cols = slice(half * (width // 2), (half + 1) * (width // 2))

        @pl.when(other == half)
        def _():
            pltpu.make_async_copy(q_six, query_o.at[:, cols], out_sem.at[4]).start()

    last(1)

    for o in offs_z:
        remote(enc.at[o], enc_in.at[o], enc_ss.at[o], enc_rs.at[o], at_z(o)).wait_send()
    for copy in (
        lv_copies + cnt_copies + score_copies + pool_copies + pool_back + lgr_copies + lga_copies
        + q_x_copies + q_h_copies + og_copies + u_core + u_x_copies[0] + u_x_copies[1]
        + [q_core, q_back, og_core]
    ):
        copy.wait_send()
    for b in range(owners):
        o, q_copy = q_y_copy(b)

        @pl.when(o != 0)
        def _():
            q_copy.wait_send()

    @pl.when(y < owners)
    def _():
        for copy in q_g_copies:
            copy.wait_send()

    for k in range(2):
        for b in range(per_core):
            o, copies = w_y_copies(k, b)
            copies[1].wait_send()

            @pl.when(o != 0)
            def _():
                copies[0].wait_send()

    for copy in out_copies:
        copy.wait()
    pltpu.make_async_copy(w_out.at[0], down_o, out_sem.at[5]).wait()
    pltpu.make_async_copy(w_out.at[1], up_o, out_sem.at[6]).wait()
    pltpu.make_async_copy(q_five, query_o.at[:, 0 : width // 2], out_sem.at[3]).wait()
    pltpu.make_async_copy(q_six, query_o.at[:, 0 : width // 2], out_sem.at[4]).wait()


def body(dims, queries, label_ids, label_text, up_weight, down_weight, free_vectors, moments, seconds):
    ny, nx, nc, nz = dims
    labels, tokens, width = label_text.shape
    units = up_weight.shape[1]
    rows = labels * tokens
    text_rows = label_text.reshape(rows, width)
    lz = labels // nz
    rows_out = width // (ny * nx * nc)
    chip_rows = rows_out * nc
    per_core = ny // nc
    half = width // 2
    qx = 192 // nx
    qy = qx // (6 if ny == 8 else ny)
    pieces = 2 if per_core % 2 == 0 else 1
    per_piece = per_core // pieces
    staged = -(-rows_out // 8) * 8
    vmem = pltpu.VMEM
    dma = pltpu.SemaphoreType.DMA
    scratch = [
        vmem((rows, width), BF16),
        vmem((width, rows), BF16),
        vmem((width, units), BF16),
        vmem((width, units), BF16),
        vmem((256, width), BF16),
        vmem((10, 192), jnp.int32),
        vmem((labels, width), F32),
        vmem((labels, width), F32),
        vmem((labels, width), F32),
        vmem((rows, units), F32),
        vmem((nx, nc, labels, units), F32),
        vmem((nx, 2 * nc * labels, units), BF16),
        vmem((nz, lz, width), F32),
        vmem((nz, lz, width), F32),
        vmem((labels, width), F32),
        vmem((labels, width), BF16),
        vmem((16, 128), F32),
        vmem((16, 128), F32),
        vmem((16, 128), F32),
        vmem((8, 128), F32),
        vmem((nz, 8, 128), F32),
        vmem((16, 128), F32),
        vmem((16, 128), F32),
        vmem((16, 128), F32),
        vmem((2, 16, 128), F32),
        vmem((nx, 16, 128), F32),
        vmem((ny, 16, 128), F32),
        vmem((labels, width), F32),
        vmem((nz, lz, width), F32),
        vmem((labels, width), F32),
        vmem((2, 192, half), F32),
        vmem((192, half), F32),
        vmem((192, half), F32),
        vmem((nx, qx, half), F32),
        vmem((qx, half), F32),
        vmem((ny, qy, half), F32),
        vmem((qx, half), F32),
        vmem((192, half), F32),
        vmem((192, half), F32),
        vmem((nc, labels, half), F32),
        vmem((per_core, nx, chip_rows, nc * labels), F32),
        vmem((nx, per_core, chip_rows, nc * labels), F32),
        vmem((rows, units), BF16),
        vmem((nc, pieces, per_piece, nx, chip_rows, units), F32),
        vmem((pieces, per_piece, nx, chip_rows, units), F32),
        vmem((pieces, per_piece, nx, chip_rows, units), F32),
        vmem((pieces, nx, per_piece, chip_rows, units), F32),
        vmem((2, per_core, chip_rows, units), F32),
        vmem((2, ny, staged, units), F32),
        vmem((2, rows_out, units), F32),
        vmem((labels, width), F32),
        vmem((labels, width), F32),
        vmem((labels, width), F32),
        dma((8,)),
        dma((nz,)),
        dma((7,)),
        dma((nz,)),
        dma((nz,)),
        dma((nz,)),
        dma((nz,)),
        dma((nz,)),
        dma((nz,)),
        dma((2 + nx + ny,)),
        dma((2 + nx + ny,)),
        dma((nz,)),
        dma((nz,)),
        dma((nz,)),
        dma((nz,)),
        dma((1 + 2 * nx + 2 * ny,)),
        dma((1 + 2 * nx + 2 * ny,)),
        dma((2 * nx,)),
        dma((2 * nx,)),
        dma((1 + nx,)),
        dma((1 + nx,)),
        dma((pieces, 1 + nx)),
        dma((pieces, 1 + nx)),
        dma((2, 2, per_core)),
        dma((2, ny)),
    ]
    hbm = pl.BlockSpec(memory_space=pl.ANY)
    flops = 2 * rows * width * units * 2
    results = pl.pallas_call(
        functools.partial(kernel, dims),
        out_shape=[
            pltpu.VMEM((labels, width), F32),
            pltpu.VMEM((labels, width), F32),
            pltpu.VMEM((labels, width), F32),
            pltpu.VMEM((192, width), F32),
            pltpu.VMEM((rows_out, units), F32),
            pltpu.VMEM((rows_out, units), F32),
        ],
        in_specs=[hbm] * 8,
        out_specs=[pl.BlockSpec(memory_space=pltpu.VMEM)] * 6,
        scratch_shapes=scratch,
        name="step",
        cost_estimate=pl.CostEstimate(flops=flops, bytes_accessed=8 * 2**20, transcendentals=rows * units),
        compiler_params=pltpu.CompilerParams(
            collective_id=0, has_side_effects=True, vmem_limit_bytes=56 * 2**20
        ),
    )(queries, label_ids.T, text_rows, up_weight, down_weight, free_vectors, moments, seconds)
    count = len(results)
    return pl.pallas_call(
        hand_over,
        out_shape=[jax.ShapeDtypeStruct(r.shape, r.dtype) for r in results],
        in_specs=[pl.BlockSpec(memory_space=pltpu.VMEM)] * count,
        out_specs=[hbm] * count,
        scratch_shapes=[dma((count,))],
        name="hand_over",
    )(*[pltpu.with_memory_space_constraint(r, pltpu.VMEM) for r in results])


def hand_over(*refs):
    count = (len(refs) - 1) // 2
    copies = [pltpu.make_async_copy(refs[i], refs[count + i], refs[-1].at[i]) for i in range(count)]
    for copy in copies:
        copy.start()
    for copy in copies:
        copy.wait()


def build(mesh, dims):
    placed = (
        P("query", None),
        P("query", None),
        P("label", None, None),
        P(None, "query"),
        P(None, "query"),
        P("label", None),
        P("label", None),
        P("label", None),
    )
    return jax.shard_map(
        functools.partial(body, dims),
        mesh=mesh,
        in_specs=placed,
        out_specs=(
            P("label", None),
            P("label", None),
            P("label", None),
            P("query", None),
            P("label", "query"),
            P("label", "query"),
        ),
        check_vma=False,
    )


def solution(mesh):
    return build(mesh, (8, 4, 2, mesh.shape["query"]))
```

```python
import functools
import math

import jax
import jax.numpy as jnp
from jax import lax
from jax.experimental import pallas as pl
from jax.experimental.pallas import tpu as pltpu
from jax.sharding import PartitionSpec as P

MESH = pl.DeviceIdType.MESH
F32 = jnp.float32
BF16 = jnp.bfloat16

beta_one = 0.9
beta_two = 0.999
adam_eps = 1e-08
learn_rate = 0.05
first_fix = 1.0 - 0.9**10
second_fix = 1.0 - 0.999**10
ROOT = math.sqrt(2.0 / math.pi)
CUBIC = 0.044715

NT = (((1,), (1,)), ((), ()))
TN = (((0,), (0,)), ((), ()))


def far_first(count):
    return sorted(range(1, count), key=lambda o: (-min(o, count - o), o))


def kernel(
    dims,
    queries_h,
    ids_h,
    text_h,
    up_h,
    down_h,
    free_h,
    mom_h,
    sec_h,
    free_o,
    mom_o,
    sec_o,
    query_o,
    up_o,
    down_o,
    text,
    text_t,
    upw,
    dnw,
    qp,
    ids,
    fre,
    mom,
    sec,
    slope,
    pool_in,
    pool_bf,
    enc,
    enc_in,
    lvec,
    lbf,
    idp,
    idt,
    idpack,
    cnt,
    cnt_in,
    sc_c,
    sc_x,
    sc_y,
    sc_c_in,
    sc_x_in,
    sc_y_in,
    lg_part,
    lg_in,
    lg,
    qt,
    q_c_in,
    q_one,
    q_x_in,
    q_two,
    q_y_in,
    q_four,
    q_five,
    q_six,
    lg_pair,
    og_t,
    og_in,
    pgrad,
    upart,
    u_c_in,
    u_one,
    u_x_in,
    w_two,
    w_y_in,
    w_out,
    free_n,
    mom_n,
    sec_n,
    in_sem,
    text_sem,
    out_sem,
    enc_ss,
    enc_rs,
    lv_ss,
    lv_rs,
    cnt_ss,
    cnt_rs,
    sc_ss,
    sc_rs,
    lgr_ss,
    lgr_rs,
    lga_ss,
    lga_rs,
    q_ss,
    q_rs,
    pool_ss,
    pool_rs,
    og_ss,
    og_rs,
    u_ss,
    u_rs,
    w_ss,
    w_rs,
):
    ny, nx, nc, nz = dims
    lab = lax.axis_index("label")
    z = lax.axis_index("query")
    y = lab // (nx * nc)
    x = (lab // nc) % nx
    c = lab % nc
    other = 1 - c
    offs_z, offs_y, offs_x = far_first(nz), far_first(ny), far_first(nx)
    labels, width = lvec.shape
    units = upw.shape[1]
    tokens = text.shape[0] // labels
    lz = labels // nz
    rows_z = text.shape[0] // nz

    def at_z(o):
        return (lab, (z + o) % nz)

    def at_y(o):
        return (((y + o) % ny * nx + x) * nc + c, z)

    def at_x(o):
        return ((y * nx + (x + o) % nx) * nc + c, z)

    def at_y_other(o):
        return (((y + o) % ny * nx + x) * nc + other, z)

    at_core = ((y * nx + x) * nc + other, z)

    barrier = pltpu.get_barrier_semaphore()
    peers = (
        [at_z(o) for o in offs_z]
        + [at_y(o) for o in offs_y]
        + [at_y_other(o) for o in offs_y]
        + [at_x(o) for o in offs_x]
        + [at_core]
    )
    for peer in peers:
        pl.semaphore_signal(barrier, inc=1, device_id=peer, device_id_type=MESH)

    def remote(src, dst, ss, rs, peer):
        return pltpu.make_async_remote_copy(
            src_ref=src,
            dst_ref=dst,
            send_sem=ss,
            recv_sem=rs,
            device_id=peer,
            device_id_type=MESH,
        )

    def offset_of(t):
        return (nz // 2 + (1 - 2 * (t % 2)) * ((t + 1) // 2)) % nz

    def text_copy(t):
        j = (z + offset_of(t)) % nz
        rows = pl.ds(pl.multiple_of(j * rows_z, rows_z), rows_z)
        return pltpu.make_async_copy(text_h.at[rows], text.at[rows], text_sem.at[t])

    in_copies = [
        pltpu.make_async_copy(src, dst, in_sem.at[i])
        for i, (src, dst) in enumerate(
            (
                (up_h, upw),
                (down_h, dnw),
                (free_h, fre),
                (ids_h, ids),
                (queries_h, qp.at[pl.ds(0, 192)]),
                (queries_h.at[pl.ds(128, 64)], qp.at[pl.ds(192, 64)]),
                (mom_h, mom),
                (sec_h, sec),
            )
        )
    ]
    in_copies[0].start()
    text_copy(0).start()
    in_copies[1].start()

    def start_text(t, carry):
        text_copy(t).start()
        return carry

    lax.fori_loop(1, nz, start_text, 0)
    for copy in in_copies[2:]:
        copy.start()
    in_copies[0].wait()

    def encode(t):
        o = offset_of(t)
        j = (z + o) % nz
        text_copy(t).wait()
        hidden = []
        for half in range(2):
            rows = pl.ds(pl.multiple_of(j * rows_z + half * (rows_z // 2), rows_z // 2), rows_z // 2)
            pre = jnp.dot(text[rows, :], upw[...], preferred_element_type=F32)
            square = pre * pre
            bent = jnp.tanh(pre * (ROOT + (ROOT * CUBIC) * square))
            gate = 0.5 + 0.5 * bent
            hidden.append(pre * gate)
            slope[rows, :] = gate + (0.5 * pre) * (1.0 - bent * bent) * (
                ROOT + (3.0 * ROOT * CUBIC) * square
            )
        hidden = jnp.concatenate(hidden, axis=0)
        mean = jnp.sum(hidden.reshape(lz, tokens, units), axis=1) * (1.0 / tokens)
        pool_in[0, c, pl.ds(pl.multiple_of(j * lz, lz), lz), :] = mean
        rest = mean - mean.astype(BF16).astype(F32)
        both = jnp.concatenate([mean, rest], axis=0).astype(BF16)
        out = lax.dot_general(both, dnw[...], NT, preferred_element_type=F32)
        enc[o] = out[:lz] + out[lz:]

    def enc_copy(t):
        o = offset_of(t)
        return remote(enc.at[o], enc_in.at[o], enc_ss.at[o], enc_rs.at[o], at_z(o))

    def encode_step(t, carry):
        encode(t)
        return carry

    def send_step(t, carry):
        enc_copy(t).start()
        return carry

    def encode_send_step(t, carry):
        encode(t)
        enc_copy(t).start()
        return carry

    early = min(2, nz - 1)
    in_copies[1].wait()
    lax.fori_loop(0, early, encode_step, 0)
    pl.semaphore_wait(barrier, len(peers))
    lax.fori_loop(0, early, send_step, 0)
    lax.fori_loop(early, nz - 1, encode_send_step, 0)
    encode(nz - 1)
    own_text = pl.ds(pl.multiple_of(z * rows_z, rows_z), rows_z)
    own_rows = pl.ds(pl.multiple_of(z * lz, lz), lz)
    text_mean = jnp.sum(text[own_text, :].astype(F32).reshape(lz, tokens, width), axis=1) * (1.0 / tokens)
    in_copies[2].wait()
    total = enc[0] + text_mean + fre[own_rows, :]
    for o in offs_z:
        remote(enc.at[o], enc_in.at[o], enc_ss.at[o], enc_rs.at[o], at_z(o)).wait_recv()
        total += enc_in[o]
    lvec[own_rows, :] = total
    lv_copies = [
        remote(lvec.at[own_rows], lvec.at[own_rows], lv_ss.at[o], lv_rs.at[o], at_z(o)) for o in offs_z
    ]
    for copy in lv_copies:
        copy.start()
    pool_copies = [remote(pool_in.at[0, c], pool_in.at[0, c], pool_ss.at[0], pool_rs.at[0], at_core)]
    pool_copies += [
        remote(pool_in.at[0, c], pool_in.at[o, c], pool_ss.at[o], pool_rs.at[o], at_x(o)) for o in offs_x
    ]
    for copy in pool_copies:
        copy.start()

    in_copies[3].wait()
    local = (ids[...] - lab * labels).astype(F32)
    idp[...] = jnp.full(idp.shape, -1.0, F32)
    idp[0:10, 0:64] = local[:, 128:192]
    idt[...] = pltpu.roll(idp[...], 64, 1)
    lane = lax.broadcasted_iota(jnp.int32, (1, 128), 1)
    idpack[...] = jnp.full(idpack.shape, -1.0, F32)
    idpack[0:10, :] = local[:, 0:128]
    for r in range(5):
        idpack[10 + r : 11 + r, :] = jnp.where(lane < 64, idp[r : r + 1, :], idt[r + 5 : r + 6, :])

    def owned(p, count):
        slots = lax.broadcasted_iota(jnp.int32, (count, 128), 0).astype(F32)
        return idpack[p : p + 1, :] == slots

    def packed(rows):
        acc = jnp.zeros((128, 128), F32)
        for p in rows:
            acc += jnp.where(owned(p, 128), 1.0, 0.0)
        return acc.astype(BF16)

    ones = jnp.ones((8, 128), BF16)
    cnt[...] = lax.dot_general(ones, packed(range(10)), NT, preferred_element_type=F32) + lax.dot_general(
        ones, packed(range(10, 15)), NT, preferred_element_type=F32
    )
    cnt_copies = [remote(cnt, cnt_in.at[o], cnt_ss.at[o], cnt_rs.at[o], at_z(o)) for o in offs_z]
    for copy in cnt_copies:
        copy.start()

    def turn(t, carry):
        rows = pl.ds(pl.multiple_of(t * 256, 256), 256)
        text_t[:, rows] = jnp.transpose(text[rows, :])
        return carry

    turns = text.shape[0] // 256
    in_copies[4].wait()
    in_copies[5].wait()

    lax.fori_loop(0, turns * 3 // 8, turn, 0)
    for copy in lv_copies:
        copy.wait_recv()
    lbf[...] = lvec[...].astype(BF16)

    similar = lax.dot_general(lbf[...], qp[...], NT, preferred_element_type=F32)
    sc_c[...] = jnp.zeros(sc_c.shape, F32)
    for p in range(15):
        block = similar[:, 0:128] if p < 10 else similar[:, 128:256]
        sc_c[p : p + 1, :] = jnp.sum(jnp.where(owned(p, labels), block, 0.0), axis=0, keepdims=True)
    score_copies = []

    def exchange(src, dst, base, offs, at, first, last):
        copies = [
            remote(src, dst.at[o], sc_ss.at[base + o], sc_rs.at[base + o], at(o)) for o in offs
        ]
        score_copies.extend(copies)
        for copy in copies:
            copy.start()
        lax.fori_loop(first, last, turn, 0)
        acc = src[...]
        for copy, o in zip(copies, offs):
            copy.wait_recv()
            acc += dst[o]
        return acc

    sc_x[...] = exchange(sc_c, sc_c_in, 0, [1], lambda o: at_core, 0, 0)
    sc_y[...] = exchange(sc_x, sc_x_in, 2, offs_x, at_x, turns * 3 // 8, turns * 5 // 8)
    scores = exchange(sc_y, sc_y_in, 2 + nx, offs_y, at_y, turns * 5 // 8, turns)

    temper = 1.0 / math.sqrt(width)
    scores = scores * temper
    top, low = scores[0:10], scores[10:15]
    top_max = jnp.max(top, axis=0, keepdims=True)
    low_max = jnp.max(low, axis=0, keepdims=True)
    low_max = jnp.maximum(low_max, pltpu.roll(low_max, 64, 1))
    top = jnp.exp(top - top_max)
    low = jnp.exp(low - low_max)
    top_sum = jnp.sum(top, axis=0, keepdims=True)
    low_sum = jnp.sum(low, axis=0, keepdims=True)
    low_sum = low_sum + pltpu.roll(low_sum, 64, 1)
    row_t = lax.broadcasted_iota(jnp.int32, (10, 128), 0)
    row_l = lax.broadcasted_iota(jnp.int32, (5, 128), 0)
    lane_l = lax.broadcasted_iota(jnp.int32, (5, 128), 1)
    top = (top / top_sum - jnp.where(row_t < 2, 0.5, 0.0)) * temper
    low = (low / low_sum - jnp.where((row_l < 2) & (lane_l < 64), 0.5, 0.0)) * temper
    top = top.astype(BF16).astype(F32)
    low = low.astype(BF16).astype(F32)
    spread = []
    for coef, base in ((top, 0), (low, 10)):
        acc = jnp.zeros((labels, 128), F32)
        for k in range(coef.shape[0]):
            acc += jnp.where(owned(base + k, labels), coef[k : k + 1], 0.0)
        spread.append(acc)
    spread = jnp.concatenate(spread, axis=1).astype(BF16)

    lg_part[...] = jnp.dot(spread, qp[...], preferred_element_type=F32)
    lgr_copies = []
    for o in offs_z:
        rows = pl.ds(pl.multiple_of((z + o) % nz * lz, lz), lz)
        lgr_copies.append(remote(lg_part.at[rows], lg_in.at[o], lgr_ss.at[o], lgr_rs.at[o], at_z(o)))
        lgr_copies[-1].start()

    terms = lax.dot_general(spread, lbf[...], TN, preferred_element_type=F32)
    for half in range(2):
        cols = slice(half * (width // 2), (half + 1) * (width // 2))
        qt[half, 0:128, :] = terms[0:128, cols]
        qt[half, 128:192, :] = terms[128:192, cols] + terms[192:256, cols]
    q_core = remote(qt.at[other], q_c_in, q_ss.at[0], q_rs.at[0], at_core)
    q_core.start()
    pool_back = []
    for copy, o in zip(pool_copies[1:], offs_x):
        copy.wait_recv()
        pool_back.append(
            remote(pool_in.at[o, c], pool_in.at[o, c], pool_ss.at[nx + o], pool_rs.at[nx + o], at_core)
        )
        pool_back[-1].start()
    qx = 192 // nx
    owners = 6 if ny == 8 else ny
    qy = qx // owners
    base_y, base_g, base_h = 1 + nx, 1 + nx + ny, 1 + nx + 2 * ny
    q_core.wait_recv()
    q_one[...] = qt[c] + q_c_in[...]
    q_x_copies = []
    for o in offs_x:
        rows = pl.ds(pl.multiple_of((x + o) % nx * qx, qx), qx)
        q_x_copies.append(remote(q_one.at[rows], q_x_in.at[o], q_ss.at[1 + o], q_rs.at[1 + o], at_x(o)))
        q_x_copies[-1].start()

    total = lg_part[own_rows, :]
    for copy, o in zip(lgr_copies, offs_z):
        copy.wait_recv()
        total += lg_in[o]
    lg[own_rows, :] = total
    lga_copies = [remote(lg.at[own_rows], lg.at[own_rows], lga_ss.at[o], lga_rs.at[o], at_z(o)) for o in offs_z]
    for copy in lga_copies:
        copy.start()

    seen = cnt[...]
    for copy, o in zip(cnt_copies, offs_z):
        copy.wait_recv()
        seen += cnt_in[o]
    diag = lax.broadcasted_iota(jnp.int32, (labels, 128), 0) == lax.broadcasted_iota(
        jnp.int32, (labels, 128), 1
    )
    touched = jnp.sum(jnp.where(diag, seen[0:1], 0.0), axis=1, keepdims=True) > 0.5

    own_x = pl.ds(pl.multiple_of(x * qx, qx), qx)
    acc = q_one[own_x, :]
    for copy, o in zip(q_x_copies, offs_x):
        copy.wait_recv()
        acc += q_x_in[o]
    q_two[...] = acc

    def q_y_copy(b):
        o = (b - y + ny) % ny
        return o, remote(
            q_two.at[pl.ds(b * qy, qy)],
            q_y_in.at[o],
            q_ss.at[base_y + b],
            q_rs.at[base_y + o],
            ((b * nx + x) * nc + c, z),
        )

    for b in range(owners):
        o, q_copy = q_y_copy(b)

        @pl.when(o != 0)
        def _():
            q_copy.start()

    pool_copies[0].wait_recv()
    for copy in pool_back:
        copy.wait_recv()
    for o in range(nx):
        for k in range(nc):
            mean = pool_in[o, k]
            whole = mean.astype(BF16)
            pool_bf[o, k * labels : (k + 1) * labels, :] = whole
            pool_bf[o, (nc + k) * labels : (nc + k + 1) * labels, :] = (mean - whole.astype(F32)).astype(BF16)

    for copy in lga_copies:
        copy.wait_recv()
    grad = lg[...]
    out_grad = grad.astype(BF16)
    hidden_grad = jnp.dot(out_grad, dnw[...], preferred_element_type=F32) * (1.0 / tokens)

    half_rows = width // nc
    cols_other = pl.ds(pl.multiple_of(other * half_rows, half_rows), half_rows)
    og_core = remote(lg.at[:, cols_other], lg_pair.at[c], og_ss.at[0], og_rs.at[0], at_core)
    og_core.start()

    lg_pair[c] = jnp.where(c == 0, grad[:, :half_rows], grad[:, half_rows:])
    for j in range(nz):
        rows = slice(j * rows_z, (j + 1) * rows_z)
        spreaded = jnp.broadcast_to(
            hidden_grad[j * lz : (j + 1) * lz, None, :], (lz, tokens, units)
        ).reshape(rows_z, units)
        pgrad[rows, :] = (slope[rows, :] * spreaded).astype(BF16)

    og_core.wait_recv()
    pair = lg_pair[...].reshape(nc * labels, half_rows).astype(BF16).astype(F32)
    og_t[...] = jnp.transpose(pair).reshape(og_t.shape)
    og_copies = []
    for o in offs_x:
        og_copies.append(
            remote(og_t.at[:, (x + o) % nx], og_in.at[o], og_ss.at[1 + o], og_rs.at[1 + o], at_x(o))
        )
        og_copies[-1].start()

    mine = pl.ds(pl.multiple_of(y % owners * qy, qy), qy)
    q_g_copies = [
        remote(q_four.at[mine], q_four.at[mine], q_ss.at[base_g + o], q_rs.at[base_g + y], at_y(o))
        for o in offs_y
    ]

    @pl.when(y < owners)
    def _():
        acc = q_two[mine, :]
        for o in offs_y:
            remote(
                q_two.at[pl.ds(0, qy)], q_y_in.at[o], q_ss.at[base_y], q_rs.at[base_y + o], at_y(o)
            ).wait_recv()
            acc += q_y_in[o]
        q_four[mine, :] = acc
        for copy in q_g_copies:
            copy.start()

    per_core = ny // nc
    pieces = 2 if per_core % 2 == 0 else 1
    per_piece = per_core // pieces
    piece_rows = half_rows // pieces

    def up_piece(h, p):
        rows = pl.ds(pl.multiple_of(h * half_rows + p * piece_rows, piece_rows), piece_rows)
        part = jnp.dot(text_t[rows, :], pgrad[...], preferred_element_type=F32)
        upart[h, p] = part.reshape(upart.shape[2:])

    u_core = []
    for p in range(pieces):
        up_piece(other, p)
        u_core.append(remote(upart.at[other, p], u_c_in.at[p], u_ss.at[p, 0], u_rs.at[p, 0], at_core))
        u_core[p].start()

    u_x_copies = [[], []]

    def across_x(p):
        u_core[p].wait_recv()
        u_one[p] = upart[c, p] + u_c_in[p]
        for o in offs_x:
            copy = remote(
                u_one.at[p, :, (x + o) % nx],
                u_x_in.at[p, o],
                u_ss.at[p, 1 + o],
                u_rs.at[p, 1 + o],
                at_x(o),
            )
            copy.start()
            u_x_copies[p].append(copy)

    for p in range(pieces):
        up_piece(c, p)
        across_x(p)

    rows_out = w_out.shape[1]
    step_rows, slice_rows = rows_out // 8 * 8, -(-rows_out // 8) * 8

    def w_y_copies(k, b):
        goal = c * per_core + b
        o = (goal - y + ny) % ny
        copies = []
        for side, core in enumerate((c, other)):
            rows = pl.ds(pl.multiple_of(core * step_rows, 8), slice_rows)
            copies.append(
                remote(
                    w_two.at[k, b, rows],
                    w_y_in.at[k, o],
                    w_ss.at[k, side, b],
                    w_rs.at[k, o],
                    ((goal * nx + x) * nc + core, z),
                )
            )
        return o, copies

    def across_y(k, b):
        o, copies = w_y_copies(k, b)
        copies[1].start()

        @pl.when(o != 0)
        def _():
            copies[0].start()

        @pl.when(o == 0)
        def _():
            w_y_in[k, 0] = w_two[k, b, pl.ds(pl.multiple_of(c * step_rows, 8), slice_rows), :]

    def down_term(values, o):
        values = values.reshape(half_rows // nx, nc * labels).astype(BF16)
        return jnp.dot(
            jnp.concatenate([values, values], axis=1), pool_bf[o], preferred_element_type=F32
        )

    acc = down_term(og_t[:, x], 0)
    for copy, o in zip(og_copies, offs_x):
        copy.wait_recv()
        acc += down_term(og_in[o], o)
    w_two[0] = acc.reshape(w_two.shape[1:])
    for b in range(per_core):
        across_y(0, b)

    for b in range(owners):

        @pl.when(y != b)
        def _():
            rows = pl.ds(b * qy, qy)
            remote(
                q_four.at[rows], q_four.at[rows], q_ss.at[base_g], q_rs.at[base_g + b], at_core
            ).wait_recv()

    q_five[own_x, :] = q_four[...]
    q_h_copies = [
        remote(q_four, q_five.at[own_x], q_ss.at[base_h + o], q_rs.at[base_h + o], at_x(o)) for o in offs_x
    ]
    for copy in q_h_copies:
        copy.start()

    def up_across_y(p):
        acc = u_one[p, :, x]
        for copy, o in zip(u_x_copies[p], offs_x):
            copy.wait_recv()
            acc += u_x_in[p, o]
        for i in range(per_piece):
            w_two[1, p * per_piece + i] = acc[i]
            across_y(1, p * per_piece + i)

    up_across_y(0)

    in_copies[6].wait()
    in_copies[7].wait()
    moment = beta_one * mom[...] + (1.0 - beta_one) * grad
    second = beta_two * sec[...] + (1.0 - beta_two) * grad * grad
    update = learn_rate * (moment / first_fix) / (jnp.sqrt(second / second_fix) + adam_eps)
    free_n[...] = jnp.where(touched, fre[...] - update, fre[...])
    mom_n[...] = jnp.where(touched, moment, mom[...])
    sec_n[...] = jnp.where(touched, second, sec[...])
    out_copies = [
        pltpu.make_async_copy(src, dst, out_sem.at[i])
        for i, (src, dst) in enumerate(((free_n, free_o), (mom_n, mom_o), (sec_n, sec_o)))
    ]
    for copy in out_copies:
        copy.start()

    for p in range(1, pieces):
        up_across_y(p)

    for copy in q_h_copies:
        copy.wait_recv()
    q_back = remote(q_five, q_six, q_ss.at[base_h], q_rs.at[base_h], at_core)
    q_back.start()

    holder = y // per_core == c

    def last(k):
        @pl.when(jnp.logical_not(holder))
        def _():
            remote(
                w_two.at[k, 0, pl.ds(0, slice_rows)], w_y_in.at[k, 0], w_ss.at[k, 0, 0], w_rs.at[k, 0], at_core
            ).wait_recv()

        for o in offs_y:
            remote(
                w_two.at[k, 0, pl.ds(0, slice_rows)], w_y_in.at[k, o], w_ss.at[k, 0, 0], w_rs.at[k, o], at_y(o)
            ).wait_recv()
        acc = w_y_in[k, 0]
        for o in range(1, ny):
            acc += w_y_in[k, o]
        shift = rows_out - step_rows
        w_out[k] = jnp.where(c == 0, acc[:rows_out], acc[shift : shift + rows_out])
        pltpu.make_async_copy(w_out.at[k], (down_o, up_o)[k], out_sem.at[5 + k]).start()

    last(0)

    for half in range(2):
        cols = slice(half * (width // 2), (half + 1) * (width // 2))

        @pl.when(c == half)
        def _():
            pltpu.make_async_copy(q_five, query_o.at[:, cols], out_sem.at[3]).start()

    q_back.wait_recv()
    for half in range(2):
        cols = slice(half * (width // 2), (half + 1) * (width // 2))

        @pl.when(other == half)
        def _():
            pltpu.make_async_copy(q_six, query_o.at[:, cols], out_sem.at[4]).start()

    last(1)

    for o in offs_z:
        remote(enc.at[o], enc_in.at[o], enc_ss.at[o], enc_rs.at[o], at_z(o)).wait_send()
    for copy in (
        lv_copies + cnt_copies + score_copies + pool_copies + pool_back + lgr_copies + lga_copies
        + q_x_copies + q_h_copies + og_copies + u_core + u_x_copies[0] + u_x_copies[1]
        + [q_core, q_back, og_core]
    ):
        copy.wait_send()
    for b in range(owners):
        o, q_copy = q_y_copy(b)

        @pl.when(o != 0)
        def _():
            q_copy.wait_send()

    @pl.when(y < owners)
    def _():
        for copy in q_g_copies:
            copy.wait_send()

    for k in range(2):
        for b in range(per_core):
            o, copies = w_y_copies(k, b)
            copies[1].wait_send()

            @pl.when(o != 0)
            def _():
                copies[0].wait_send()

    for copy in out_copies:
        copy.wait()
    pltpu.make_async_copy(w_out.at[0], down_o, out_sem.at[5]).wait()
    pltpu.make_async_copy(w_out.at[1], up_o, out_sem.at[6]).wait()
    pltpu.make_async_copy(q_five, query_o.at[:, 0 : width // 2], out_sem.at[3]).wait()
    pltpu.make_async_copy(q_six, query_o.at[:, 0 : width // 2], out_sem.at[4]).wait()


def body(dims, queries, label_ids, label_text, up_weight, down_weight, free_vectors, moments, seconds):
    ny, nx, nc, nz = dims
    labels, tokens, width = label_text.shape
    units = up_weight.shape[1]
    rows = labels * tokens
    text_rows = label_text.reshape(rows, width)
    lz = labels // nz
    rows_out = width // (ny * nx * nc)
    chip_rows = rows_out * nc
    per_core = ny // nc
    half = width // 2
    qx = 192 // nx
    qy = qx // (6 if ny == 8 else ny)
    pieces = 2 if per_core % 2 == 0 else 1
    per_piece = per_core // pieces
    staged = -(-rows_out // 8) * 8
    vmem = pltpu.VMEM
    dma = pltpu.SemaphoreType.DMA
    scratch = [
        vmem((rows, width), BF16),
        vmem((width, rows), BF16),
        vmem((width, units), BF16),
        vmem((width, units), BF16),
        vmem((256, width), BF16),
        vmem((10, 192), jnp.int32),
        vmem((labels, width), F32),
        vmem((labels, width), F32),
        vmem((labels, width), F32),
        vmem((rows, units), F32),
        vmem((nx, nc, labels, units), F32),
        vmem((nx, 2 * nc * labels, units), BF16),
        vmem((nz, lz, width), F32),
        vmem((nz, lz, width), F32),
        vmem((labels, width), F32),
        vmem((labels, width), BF16),
        vmem((16, 128), F32),
        vmem((16, 128), F32),
        vmem((16, 128), F32),
        vmem((8, 128), F32),
        vmem((nz, 8, 128), F32),
        vmem((16, 128), F32),
        vmem((16, 128), F32),
        vmem((16, 128), F32),
        vmem((2, 16, 128), F32),
        vmem((nx, 16, 128), F32),
        vmem((ny, 16, 128), F32),
        vmem((labels, width), F32),
        vmem((nz, lz, width), F32),
        vmem((labels, width), F32),
        vmem((2, 192, half), F32),
        vmem((192, half), F32),
        vmem((192, half), F32),
        vmem((nx, qx, half), F32),
        vmem((qx, half), F32),
        vmem((ny, qy, half), F32),
        vmem((qx, half), F32),
        vmem((192, half), F32),
        vmem((192, half), F32),
        vmem((nc, labels, half), F32),
        vmem((per_core, nx, chip_rows, nc * labels), F32),
        vmem((nx, per_core, chip_rows, nc * labels), F32),
        vmem((rows, units), BF16),
        vmem((nc, pieces, per_piece, nx, chip_rows, units), F32),
        vmem((pieces, per_piece, nx, chip_rows, units), F32),
        vmem((pieces, per_piece, nx, chip_rows, units), F32),
        vmem((pieces, nx, per_piece, chip_rows, units), F32),
        vmem((2, per_core, chip_rows, units), F32),
        vmem((2, ny, staged, units), F32),
        vmem((2, rows_out, units), F32),
        vmem((labels, width), F32),
        vmem((labels, width), F32),
        vmem((labels, width), F32),
        dma((8,)),
        dma((nz,)),
        dma((7,)),
        dma((nz,)),
        dma((nz,)),
        dma((nz,)),
        dma((nz,)),
        dma((nz,)),
        dma((nz,)),
        dma((2 + nx + ny,)),
        dma((2 + nx + ny,)),
        dma((nz,)),
        dma((nz,)),
        dma((nz,)),
        dma((nz,)),
        dma((1 + 2 * nx + 2 * ny,)),
        dma((1 + 2 * nx + 2 * ny,)),
        dma((2 * nx,)),
        dma((2 * nx,)),
        dma((1 + nx,)),
        dma((1 + nx,)),
        dma((pieces, 1 + nx)),
        dma((pieces, 1 + nx)),
        dma((2, 2, per_core)),
        dma((2, ny)),
    ]
    hbm = pl.BlockSpec(memory_space=pl.ANY)
    flops = 2 * rows * width * units * 2
    results = pl.pallas_call(
        functools.partial(kernel, dims),
        out_shape=[
            pltpu.VMEM((labels, width), F32),
            pltpu.VMEM((labels, width), F32),
            pltpu.VMEM((labels, width), F32),
            pltpu.VMEM((192, width), F32),
            pltpu.VMEM((rows_out, units), F32),
            pltpu.VMEM((rows_out, units), F32),
        ],
        in_specs=[hbm] * 8,
        out_specs=[pl.BlockSpec(memory_space=pltpu.VMEM)] * 6,
        scratch_shapes=scratch,
        name="step",
        cost_estimate=pl.CostEstimate(flops=flops, bytes_accessed=8 * 2**20, transcendentals=rows * units),
        compiler_params=pltpu.CompilerParams(
            collective_id=0, has_side_effects=True, vmem_limit_bytes=56 * 2**20
        ),
    )(queries, label_ids.T, text_rows, up_weight, down_weight, free_vectors, moments, seconds)
    count = len(results)
    return pl.pallas_call(
        hand_over,
        out_shape=[jax.ShapeDtypeStruct(r.shape, r.dtype) for r in results],
        in_specs=[pl.BlockSpec(memory_space=pltpu.VMEM)] * count,
        out_specs=[hbm] * count,
        scratch_shapes=[dma((count,))],
        name="hand_over",
    )(*[pltpu.with_memory_space_constraint(r, pltpu.VMEM) for r in results])


def hand_over(*refs):
    count = (len(refs) - 1) // 2
    copies = [pltpu.make_async_copy(refs[i], refs[count + i], refs[-1].at[i]) for i in range(count)]
    for copy in copies:
        copy.start()
    for copy in copies:
        copy.wait()


def build(mesh, dims):
    placed = (
        P("query", None),
        P("query", None),
        P("label", None, None),
        P(None, "query"),
        P(None, "query"),
        P("label", None),
        P("label", None),
        P("label", None),
    )
    return jax.shard_map(
        functools.partial(body, dims),
        mesh=mesh,
        in_specs=placed,
        out_specs=(
            P("label", None),
            P("label", None),
            P("label", None),
            P("query", None),
            P("label", "query"),
            P("label", "query"),
        ),
        check_vma=False,
    )


def solution(mesh):
    return build(mesh, (8, 4, 2, mesh.shape["query"]))
```
